128 devices in a mesh: seq: 32 (over x, z, core), head: 4 (over y).
Axes of the slice: x: 4, y: 4, z: 4, core: 2. Of those that a mesh axis runs over, the one named last changes fastest.
Arguments:
- values: bfloat16 [32768, 8192], P('seq', 'head'), may hold values from -0.0625 to 0.0625
- writes: bfloat16 [32768, 128], P('seq'), may hold values from -0.5 to 0.5
- reads: bfloat16 [32768, 128], P('seq'), may hold values from -0.5 to 0.5
- out_grad: bfloat16 [32768, 8192], P('seq', 'head'), may hold values from -0.375 to 0.375
- log_decay: float32 [128, 32768], P('head', 'seq'), may hold values from -2 to 0, as said below
- starting_head_state: float32 [128, 8192], P('head'), may hold values from -1.5 to 1.5
Outputs:
- values_grad: bfloat16 [32768, 8192], P('seq', 'head')
- writes_grad: float32 [32768, 128], P('seq')
- reads_grad: float32 [32768, 128], P('seq')
- initial_grad: float32 [128, 8192], P('head')
The draws below stay inside these ranges and needn't reach their ends.
Inputs may be any that keep to these rules, and one draw needn't show every extreme that they name: `log_decay`: each entry is the logarithm of a head's decay factor at a position.
All inputs are finite; a program needn't handle non-finite values.
Results may differ from the reference program's by a relative error of at most 0.0013.
Values sent between devices are 32-bit elements; how exact they have to be, the bound alone decides.
A program may use at most 256 MiB of HBM per device.

```python
import math
import jax
import jax.numpy as jnp
from jax import lax

HEADS = 128
HEAD_DIM = 64
D_STATE = 128
TOK_DEV = 1024
SEQ = 32768


def draw_log_decay(key, part):
    keys = jax.random.split(key, 8)
    fast_count = HEADS // 4
    middle_count = HEADS // 4
    head_rank = jax.random.permutation(keys[0], HEADS)[:, None]
    slow_rate = jnp.exp(jax.random.uniform(keys[1], (HEADS, 1), jnp.float32, math.log(0.1), math.log(1.5))) / SEQ
    fast_rate = jnp.exp(jax.random.uniform(keys[2], (HEADS, 1), jnp.float32, math.log(1.0 / 50.0), math.log(1.0 / 30.0)))
    middle_rate = jnp.exp(jax.random.uniform(keys[7], (HEADS, 1), jnp.float32, math.log(1.0), math.log(2.5))) / TOK_DEV
    fading_speed = jnp.where(head_rank < fast_count, fast_rate, jnp.where(head_rank < fast_count + middle_count, middle_rate, slow_rate))
    rough_approximation = jnp.exp(jax.random.uniform(keys[3], (HEADS, SEQ), jnp.float32, math.log(0.5), math.log(2.0)))
    symbol_window = jnp.exp(jax.random.uniform(keys[4], (HEADS, 16, 1), jnp.float32, math.log(0.5), math.log(2.0)))
    symbol_window = jnp.broadcast_to(symbol_window, (HEADS, 16, SEQ // 16)).reshape(HEADS, SEQ)
    spots = jax.random.randint(keys[5], (3,), 0, SEQ)
    objective_numbers = jax.random.uniform(keys[6], (HEADS, 3), jnp.float32, 0.5, 0.8)
    agreement_tally = (jnp.arange(SEQ)[None, :, None] == spots[None, None, :]).astype(jnp.float32)
    batch_clusters = jnp.sum(agreement_tally * jnp.log(objective_numbers)[:, None, :], axis=2)
    return (-fading_speed * rough_approximation * symbol_window + batch_clusters).astype(jnp.float32)


def levels(rng, dims, cuts, smallest, top_value):
    factor_of, own = 1.0, jax.random.fold_in(rng, 6)
    for axis_at, shards_of in cuts:
        steps = jnp.exp(jax.random.uniform(jax.random.fold_in(own, axis_at), (shards_of,), jnp.float32, smallest / len(cuts), top_value / len(cuts)))
        factor_of = factor_of * jnp.repeat(steps, dims[axis_at] // shards_of).reshape([-1 if axis == axis_at else 1 for axis in range(len(dims))])
    return factor_of


def centred(rng, shape, scale, bound, pieces=(), held_as=jnp.bfloat16):
    gain = levels(rng, shape, pieces, -0.22, 0.18) if pieces else 1.0
    array = jax.random.normal(rng, shape, jnp.float32) * scale * gain
    return jnp.minimum(jnp.maximum(array, -bound), bound).astype(held_as)


def setup_inputs(seed: int = 0) -> dict:
    splits = jax.random.split(jax.random.key(seed), 7)
    values = centred(splits[0], (SEQ, HEADS * HEAD_DIM), (HEADS * HEAD_DIM) ** -0.5, 0.0625, ((0, 32), (1, 4)))
    writes = centred(splits[1], (SEQ, D_STATE), D_STATE ** -0.5, 0.5, ((0, 32),))
    reads = centred(splits[2], (SEQ, D_STATE), D_STATE ** -0.5, 0.5, ((0, 32),))
    out_grad = centred(splits[3], (SEQ, HEADS * HEAD_DIM), (SEQ // D_STATE) ** -0.5, 0.375, ((0, 32), (1, 4)))
    log_decay = draw_log_decay(jax.random.fold_in(splits[6], 71), 0)
    starting_head_state = centred(splits[5], (HEADS, HEAD_DIM * D_STATE), 0.25, 1.5, ((0, 4),), jnp.float32)
    return {"values": values, "writes": writes, "reads": reads, "out_grad": out_grad, "log_decay": log_decay, "starting_head_state": starting_head_state}


def reference(values, writes, reads, out_grad, log_decay, starting_head_state):
    highest = lax.Precision.HIGHEST
    total_len = values.shape[0]
    head_count = log_decay.shape[0]
    block_size = min(256, total_len)
    block_count = total_len // block_size
    block_values = values.reshape(block_count, block_size, head_count, HEAD_DIM)
    block_grads = out_grad.reshape(block_count, block_size, head_count, HEAD_DIM)
    block_writes = writes.reshape(block_count, block_size, D_STATE)
    block_reads = reads.reshape(block_count, block_size, D_STATE)
    block_logs = log_decay.reshape(head_count, block_count, block_size).transpose(1, 0, 2)
    first_state = starting_head_state.reshape(head_count, HEAD_DIM, D_STATE)

    def forward_step(state_now, block):
        part_values, part_writes, part_logs = block
        cumulative = jnp.cumsum(part_logs, axis=1)
        block_total = cumulative[:, -1]
        to_end = jnp.exp(block_total[:, None] - cumulative).T[:, :, None]
        rescaled_quantities = part_values.astype(jnp.float32) * to_end
        fresh_state = jnp.einsum('jhp,jn->hpn', rescaled_quantities, part_writes.astype(jnp.float32), precision=highest)
        return jnp.exp(block_total)[:, None, None] * state_now + fresh_state, state_now

    final_state, starts = lax.scan(forward_step, first_state, (block_values, block_writes, block_logs))

    def backward_step(after_end, block):
        part_values, part_grads, part_writes, part_reads, part_logs, start_state = block
        values_wide = part_values.astype(jnp.float32)
        grads_wide = part_grads.astype(jnp.float32)
        writes_wide = part_writes.astype(jnp.float32)
        reads_wide = part_reads.astype(jnp.float32)
        cumulative = jnp.cumsum(part_logs, axis=1)
        block_total = cumulative[:, -1]
        to_end = jnp.exp(block_total[:, None] - cumulative).T[:, :, None]
        from_start = jnp.exp(cumulative).T[:, :, None]
        log_gaps = cumulative[:, :, None] - cumulative[:, None, :]
        causal = jnp.arange(block_size)[:, None] >= jnp.arange(block_size)[None, :]
        decay_mask = jnp.exp(jnp.where(causal[None], log_gaps, -1e30))
        intersections = jnp.dot(reads_wide, writes_wide.T, precision=highest)
        products = jnp.einsum('shp,ihp->hsi', grads_wide, values_wide, precision=highest)
        mixed_sums = jnp.sum(products * decay_mask, axis=0)
        rescaled_quantities = values_wide * to_end
        scaled_grads = grads_wide * from_start
        grad_values = jnp.einsum('hsi,shp->ihp', intersections[None] * decay_mask, grads_wide, precision=highest)
        grad_values = grad_values + jnp.einsum('in,hpn->ihp', writes_wide, after_end, precision=highest) * to_end
        grad_writes = jnp.dot(mixed_sums.T, reads_wide, precision=highest)
        grad_writes = grad_writes + jnp.einsum('ihp,hpn->in', rescaled_quantities, after_end, precision=highest)
        read_gradient = jnp.dot(mixed_sums, writes_wide, precision=highest)
        read_gradient = read_gradient + jnp.einsum('shp,hpn->sn', scaled_grads, start_state, precision=highest)
        carried = jnp.einsum('shp,sn->hpn', scaled_grads, reads_wide, precision=highest)
        new_after = carried + jnp.exp(block_total)[:, None, None] * after_end
        return new_after, (grad_values, grad_writes, read_gradient)

    zero_after = jnp.zeros((head_count, HEAD_DIM, D_STATE), jnp.float32)
    start_grad, outputs = lax.scan(backward_step, zero_after, (block_values, block_grads, block_writes, block_reads, block_logs, starts), reverse=True)
    grad_values, grad_writes, read_gradient = outputs
    values_grad = grad_values.reshape(total_len, head_count * HEAD_DIM).astype(jnp.bfloat16)
    writes_grad = grad_writes.reshape(total_len, D_STATE)
    reads_grad = read_gradient.reshape(total_len, D_STATE)
    initial_grad = start_grad.reshape(head_count, HEAD_DIM * D_STATE)
    return (values_grad, writes_grad, reads_grad, initial_grad)
```

```python
import functools

import jax
import jax.numpy as jnp
from jax import lax
from jax.experimental import pallas as pl
from jax.experimental.pallas import tpu as pltpu
from jax.sharding import PartitionSpec as P

HEAD_DIM = 64
D_STATE = 128
CHUNK = 128

MESH = pl.DeviceIdType.MESH
F32 = jnp.float32
BF16 = jnp.bfloat16
NN = (((1,), (0,)), ((), ()))
NT = (((1,), (1,)), ((), ()))
TN = (((0,), (0,)), ((), ()))
VMEM_LIMIT = 56 * 1024 * 1024


def dot(a, b, dims=NN):
    return lax.dot_general(a, b, dims, preferred_element_type=F32)


def split2(a):
    hi = a.astype(BF16)
    return hi, (a - hi.astype(F32)).astype(BF16)


def split3(a):
    hi = a.astype(BF16)
    rest = a - hi.astype(F32)
    mid = rest.astype(BF16)
    return hi, mid, (rest - mid.astype(F32)).astype(BF16)


def iota(shape, dim):
    return lax.broadcasted_iota(jnp.int32, shape, dim)


def spread_matrix(copies, heads):
    shape = (copies * heads, heads * HEAD_DIM)
    row = lax.rem(iota(shape, 0), heads)
    return (row == iota(shape, 1) // HEAD_DIM).astype(F32).astype(BF16)


def spread2(a, matrix):
    return dot(jnp.concatenate(split2(a), axis=1), matrix)


def local_kernel(values, writes, grads, reads, logs, state, adjoint, total, later, sooner):
    step = pl.program_id(0)
    tokens = values.shape[0]
    heads = logs.shape[0]
    steps = pl.num_programs(0)
    spread = spread_matrix(2, heads)
    first = pl.multiple_of(step * tokens, tokens)

    @pl.when(step == 0)
    def _():
        state[...] = jnp.zeros_like(state)
        adjoint[...] = jnp.zeros_like(adjoint)
        size = 256
        row, col = iota((size, size), 0), iota((size, size), 1)
        after = (col > row).astype(F32).astype(BF16)
        upto = (col <= row).astype(F32).astype(BF16)
        ones = jnp.ones((8, size), BF16)
        count = later.shape[0] // size
        parts = [split3(logs[:, k * size : (k + 1) * size]) for k in range(count)]
        sums = [sum(dot(ones, p, NT) for p in part) for part in parts]
        before = jnp.zeros((1, heads), F32)
        for k in range(count):
            sooner[k * size : (k + 1) * size, :] = jnp.exp(sum(dot(upto, p, NT) for p in parts[k]) + before)
            before = before + sums[k][:1]
        behind = jnp.zeros((1, heads), F32)
        for k in reversed(range(count)):
            later[k * size : (k + 1) * size, :] = jnp.exp(sum(dot(after, p, NT) for p in parts[k]) + behind)
            behind = behind + sums[k][:1]
        matrix = spread[:heads]
        whole = jnp.broadcast_to(before, (8, heads))
        total[...] = sum(dot(p, matrix) for p in split3(whole))

    rows = pl.ds(first, tokens)
    scaled = values[...].astype(F32) * spread2(later[rows, :], spread)
    hi, lo = split2(scaled)
    state[...] += dot(writes[...], hi, TN) + dot(writes[...], lo, TN)
    scaled = grads[...].astype(F32) * spread2(sooner[rows, :], spread)
    hi, lo = split2(scaled)
    adjoint[...] += dot(reads[...], hi, TN) + dot(reads[...], lo, TN)


def local_part(values, writes, reads, grads, logs):
    tokens, width = values.shape
    heads = logs.shape[0]
    size = 256
    wide = pl.BlockSpec((size, width), lambda k: (k, 0))
    thin = pl.BlockSpec((size, D_STATE), lambda k: (k, 0))
    whole = lambda shape: pl.BlockSpec(shape, lambda k: (0, 0))
    return pl.pallas_call(
        local_kernel,
        grid=(tokens // size,),
        in_specs=[wide, thin, wide, thin, whole((heads, tokens))],
        out_specs=[whole((D_STATE, width)), whole((D_STATE, width)), whole((8, width))],
        out_shape=[
            jax.ShapeDtypeStruct((D_STATE, width), F32),
            jax.ShapeDtypeStruct((D_STATE, width), F32),
            jax.ShapeDtypeStruct((8, width), F32),
        ],
        scratch_shapes=[pltpu.VMEM((tokens, heads), F32), pltpu.VMEM((tokens, heads), F32)],
        compiler_params=pltpu.CompilerParams(vmem_limit_bytes=VMEM_LIMIT),
        cost_estimate=pl.CostEstimate(flops=2 * 2**30, bytes_accessed=12 * 2**20, transcendentals=0),
        name="local_part",
    )(values, writes, grads, reads, logs)


def scan_kernel(
    state, adjoint, total, start, entering, leaving, initial,
    near_state, near_adjoint, near_total, outgoing, incoming, replies, answers, mine, theirs,
    near_send, near_recv, out_send, out_recv, back_send, back_recv, last_send, last_recv,
):
    chips = incoming.shape[0]
    half = D_STATE // 2
    seq = lax.axis_index("seq")
    chip = seq // 2
    core = lax.rem(seq, 2)
    partner = {"seq": chip * 2 + 1 - core}
    lanes = 2 * HEAD_DIM

    barrier = pltpu.get_barrier_semaphore()
    for turn in range(1, chips):
        other = lax.rem(chip + turn, chips)
        pl.semaphore_signal(barrier, inc=1, device_id={"seq": other * 2 + core}, device_id_type=MESH)
    pl.semaphore_signal(barrier, inc=1, device_id=partner, device_id_type=MESH)
    pl.semaphore_wait(barrier, chips)

    own = pl.ds(pl.multiple_of(core * half, half), half)
    others = pl.ds(pl.multiple_of((1 - core) * half, half), half)
    nears = []
    for k, (source, target) in enumerate(
        ((state.at[others, :], near_state), (adjoint.at[others, :], near_adjoint), (total, near_total))
    ):
        copy = pltpu.make_async_remote_copy(
            src_ref=source, dst_ref=target, send_sem=near_send.at[k], recv_sem=near_recv.at[k],
            device_id=partner, device_id_type=MESH,
        )
        copy.start()
        nears.append(copy)
    for copy in nears:
        copy.wait()

    is_first = core == 0
    outs = []
    for turn in range(chips):
        target = lax.rem(chip + turn, chips)
        cols = pl.ds(pl.multiple_of(target * lanes, lanes), lanes)
        own_log, near_log = total[:, cols], near_total[:, cols]
        log_first = jnp.where(is_first, own_log, near_log)
        log_second = jnp.where(is_first, near_log, own_log)
        own_state, far_state = state[own, cols], near_state[:, cols]
        own_adjoint, far_adjoint = adjoint[own, cols], near_adjoint[:, cols]
        state_first = jnp.where(is_first, own_state, far_state)
        state_second = jnp.where(is_first, far_state, own_state)
        adjoint_first = jnp.where(is_first, own_adjoint, far_adjoint)
        adjoint_second = jnp.where(is_first, far_adjoint, own_adjoint)
        joined_state = jnp.exp(log_second[:1]) * state_first + state_second
        joined_adjoint = adjoint_first + jnp.exp(log_first[:1]) * adjoint_second
        place = incoming.at[chip] if turn == 0 else outgoing.at[target]
        place[0:half, :] = joined_state
        place[half : 2 * half, :] = joined_adjoint
        place[2 * half :, :] = log_first + log_second
        if turn:
            copy = pltpu.make_async_remote_copy(
                src_ref=outgoing.at[target], dst_ref=incoming.at[chip],
                send_sem=out_send.at[turn], recv_sem=out_recv.at[chip],
                device_id={"seq": target * 2 + core}, device_id_type=MESH,
            )
            copy.start()
            outs.append(copy)
    for turn in range(1, chips):
        source = lax.rem(chip + turn, chips)
        pltpu.make_async_remote_copy(
            src_ref=outgoing.at[source], dst_ref=incoming.at[source],
            send_sem=out_send.at[turn], recv_sem=out_recv.at[source],
            device_id={"seq": source * 2 + core}, device_id_type=MESH,
        ).wait_recv()

    carry = start[...]
    for k in range(chips):
        replies[k, 0:half, :] = carry
        carry = jnp.exp(incoming[k, 2 * half : 2 * half + 1, :]) * carry + incoming[k, 0:half, :]
    carry = jnp.zeros((half, lanes), F32)
    for k in reversed(range(chips)):
        replies[k, half:, :] = carry
        carry = jnp.exp(incoming[k, 2 * half : 2 * half + 1, :]) * carry + incoming[k, half : 2 * half, :]
    initial[...] = carry

    backs = []
    for turn in range(1, chips):
        target = lax.rem(chip + turn, chips)
        copy = pltpu.make_async_remote_copy(
            src_ref=replies.at[target], dst_ref=answers.at[chip],
            send_sem=back_send.at[turn], recv_sem=back_recv.at[chip],
            device_id={"seq": target * 2 + core}, device_id_type=MESH,
        )
        copy.start()
        backs.append(copy)
    for turn in range(chips):
        source = lax.rem(chip + turn, chips)
        if turn:
            pltpu.make_async_remote_copy(
                src_ref=replies.at[source], dst_ref=answers.at[source],
                send_sem=back_send.at[turn], recv_sem=back_recv.at[source],
                device_id={"seq": source * 2 + core}, device_id_type=MESH,
            ).wait_recv()
            answer = answers.at[source]
        else:
            answer = replies.at[chip]
        cols = pl.ds(pl.multiple_of(source * lanes, lanes), lanes)
        came, goes = answer[0:half, :], answer[half:, :]
        own_log, near_log = total[:1, cols], near_total[:1, cols]
        moved_state = jnp.where(
            is_first, jnp.exp(own_log) * came + state[own, cols], jnp.exp(near_log) * came + near_state[:, cols]
        )
        moved_adjoint = jnp.where(
            is_first, jnp.exp(near_log) * goes + near_adjoint[:, cols], jnp.exp(own_log) * goes + adjoint[own, cols]
        )
        mine[0, :, cols] = jnp.where(is_first, came, moved_state)
        mine[1, :, cols] = jnp.where(is_first, moved_adjoint, goes)
        theirs[0, :, cols] = jnp.where(is_first, moved_state, came)
        theirs[1, :, cols] = jnp.where(is_first, goes, moved_adjoint)

    lasts = []
    for k, target in enumerate((entering, leaving)):
        copy = pltpu.make_async_remote_copy(
            src_ref=theirs.at[k], dst_ref=target.at[own, :], send_sem=last_send.at[k], recv_sem=last_recv.at[k],
            device_id=partner, device_id_type=MESH,
        )
        copy.start()
        lasts.append(copy)
    entering[own, :] = mine[0]
    leaving[own, :] = mine[1]
    for copy in outs + backs:
        copy.wait_send()
    for copy in lasts:
        copy.wait()


def scan_part(state, adjoint, total, start, chips):
    width = state.shape[1]
    half = D_STATE // 2
    lanes = 2 * HEAD_DIM
    vmem = pl.BlockSpec(memory_space=pltpu.VMEM)
    dma = pltpu.SemaphoreType.DMA
    return pl.pallas_call(
        scan_kernel,
        in_specs=[vmem] * 4,
        out_specs=[vmem] * 3,
        out_shape=[
            jax.ShapeDtypeStruct((D_STATE, width), F32),
            jax.ShapeDtypeStruct((D_STATE, width), F32),
            jax.ShapeDtypeStruct((half, lanes), F32),
        ],
        scratch_shapes=[
            pltpu.VMEM((half, width), F32),
            pltpu.VMEM((half, width), F32),
            pltpu.VMEM((8, width), F32),
            pltpu.VMEM((chips, 2 * half + 8, lanes), F32),
            pltpu.VMEM((chips, 2 * half + 8, lanes), F32),
            pltpu.VMEM((chips, 2 * half, lanes), F32),
            pltpu.VMEM((chips, 2 * half, lanes), F32),
            pltpu.VMEM((2, half, width), F32),
            pltpu.VMEM((2, half, width), F32),
            dma((3,)), dma((3,)), dma((chips,)), dma((chips,)), dma((chips,)), dma((chips,)), dma((2,)), dma((2,)),
        ],
        compiler_params=pltpu.CompilerParams(collective_id=0, has_side_effects=True, vmem_limit_bytes=VMEM_LIMIT),
        cost_estimate=pl.CostEstimate(flops=2**22, bytes_accessed=5 * 2**20, transcendentals=0),
        name="scan_part",
    )(state, adjoint, total, start)


def gradient_kernel(
    values, writes, grads, reads, logs, entering, leaving, values_grad, writes_grad, reads_grad,
    now, scaled_hi, scaled_lo, carried, inner, inner_writes, ends, sums,
):
    step = pl.program_id(0)
    steps = pl.num_programs(0)
    count = steps // 2
    size, width = values.shape
    heads = logs.shape[0]
    pairs = heads // 2
    lanes = 2 * HEAD_DIM
    spread = spread_matrix(2, heads)

    @pl.when(step == 0)
    def _():
        now[...] = entering[...]

    @pl.when(step == count)
    def _():
        now[...] = leaving[...]

    @pl.when(step < count)
    def _():
        row, col = iota((size, size), 0), iota((size, size), 1)
        upto = (col <= row).astype(F32).astype(BF16)
        chunk_logs = logs[:, pl.ds(pl.multiple_of(step * size, size), size)]
        parts = split3(chunk_logs)
        by_row = sum(dot(upto, p, NT) for p in parts)
        by_col = sum(dot(p, upto, NT) for p in parts)
        last = by_row[size - 1 :, :]
        to_end = jnp.exp(last - by_row)
        sums[step, :, :] = sum(dot(p, spread[:heads]) for p in split3(jnp.broadcast_to(last, (8, heads))))
        ends[step, :, :] = to_end
        growth = jnp.exp(sums[step, 0:1, :])
        x, g, b, c = values[...], grads[...], writes[...], reads[...]

        x_hi, x_lo = split2(x.astype(F32) * spread2(to_end, spread))
        g_hi, g_lo = split2(g.astype(F32) * spread2(jnp.exp(by_row), spread))
        scaled_hi[step, :, :] = x_hi
        scaled_lo[step, :, :] = x_lo
        carried[step, :, :] = dot(c, g_hi, TN) + dot(c, g_lo, TN)
        s_hi, s_lo = split2(now[...])
        outer = dot(g_hi, s_hi, NT) + dot(g_hi, s_lo, NT) + dot(g_lo, s_hi, NT)
        now[...] = growth * now[...] + dot(b, x_hi, TN) + dot(b, x_lo, TN)

        causal = col >= row
        meets = jnp.where(causal, dot(b, c, NT), 0.0)
        mixed = jnp.zeros((size, size), F32)
        low = iota((size, lanes), 1) < HEAD_DIM
        for q in range(pairs):
            cols = slice(q * lanes, (q + 1) * lanes)
            gp = g[:, cols]
            zero = jnp.zeros_like(gp)
            stacked = jnp.concatenate([jnp.where(low, gp, zero), jnp.where(low, zero, gp)], axis=0)
            product = dot(x[:, cols], stacked, NT)
            his, los = [], []
            for e in range(2):
                h = 2 * q + e
                decay = jnp.exp(jnp.minimum(by_col[h : h + 1, :] - by_row[:, h : h + 1], 0.0))
                mixed = mixed + product[:, e * size : (e + 1) * size] * decay
                hi, lo = split2(meets * decay)
                his.append(hi)
                los.append(lo)
            inner[step, :, cols] = dot(jnp.concatenate(his, axis=1), stacked) + dot(
                jnp.concatenate(los, axis=1), stacked
            )
        mixed = jnp.where(causal, mixed, 0.0)
        hi, lo = split2(mixed)
        inner_writes[step, :, :] = dot(hi, c) + dot(lo, c)
        hi, lo = split2(mixed.T)
        reads_grad[...] = outer + dot(hi, b) + dot(lo, b)

    @pl.when(step >= count)
    def _():
        k = steps - 1 - step
        l_hi, l_lo = split2(now[...])
        x_hi, x_lo = scaled_hi[k], scaled_lo[k]
        writes_grad[...] = (
            inner_writes[k] + dot(x_hi, l_hi, NT) + dot(x_hi, l_lo, NT) + dot(x_lo, l_hi, NT)
        )
        b = writes[pl.ds(pl.multiple_of(k * size, size), size), :] if writes.shape[0] != size else writes[...]
        outer = (dot(b, l_hi) + dot(b, l_lo)) * spread2(ends[k], spread)
        values_grad[...] = (inner[k] + outer).astype(BF16)
        now[...] = jnp.exp(sums[k, 0:1, :]) * now[...] + carried[k]


def gradient_part(values, writes, reads, grads, logs, entering, leaving):
    tokens, width = values.shape
    heads = logs.shape[0]
    size = CHUNK
    count = tokens // size
    ahead = lambda k: (jnp.minimum(k, count - 1), 0)
    both = lambda k: (jnp.minimum(k, 2 * count - 1 - k), 0)
    back = lambda k: (jnp.minimum(count - 1, 2 * count - 1 - k), 0)
    whole = lambda shape: pl.BlockSpec(shape, lambda k: (0, 0))
    return pl.pallas_call(
        gradient_kernel,
        grid=(2 * count,),
        in_specs=[
            pl.BlockSpec((size, width), ahead),
            pl.BlockSpec((size, D_STATE), both),
            pl.BlockSpec((size, width), ahead),
            pl.BlockSpec((size, D_STATE), ahead),
            whole((heads, tokens)),
            whole((D_STATE, width)),
            whole((D_STATE, width)),
        ],
        out_specs=[
            pl.BlockSpec((size, width), back),
            pl.BlockSpec((size, D_STATE), back),
            pl.BlockSpec((size, D_STATE), ahead),
        ],
        out_shape=[
            jax.ShapeDtypeStruct((tokens, width), BF16),
            jax.ShapeDtypeStruct((tokens, D_STATE), F32),
            jax.ShapeDtypeStruct((tokens, D_STATE), F32),
        ],
        scratch_shapes=[
            pltpu.VMEM((D_STATE, width), F32),
            pltpu.VMEM((count, size, width), BF16),
            pltpu.VMEM((count, size, width), BF16),
            pltpu.VMEM((count, D_STATE, width), F32),
            pltpu.VMEM((count, size, width), F32),
            pltpu.VMEM((count, size, D_STATE), F32),
            pltpu.VMEM((count, size, heads), F32),
            pltpu.VMEM((count, 8, width), F32),
        ],
        compiler_params=pltpu.CompilerParams(vmem_limit_bytes=VMEM_LIMIT),
        cost_estimate=pl.CostEstimate(flops=16 * 2**30, bytes_accessed=20 * 2**20, transcendentals=0),
        name="gradient_part",
    )(values, writes, grads, reads, logs, entering, leaving)


def sum_kernel(
    writes_part, reads_part, block, writes_out, reads_out, initial_out,
    total, arrived, blocks, whole,
    send, recv, spread_send, spread_recv, near_send, near_recv,
):
    chips = blocks.shape[0]
    rows = writes_part.shape[0]
    half, quarter = rows // 2, rows // 4
    lanes = 2 * HEAD_DIM
    rank = lax.axis_index("head")
    seq = lax.axis_index("seq")
    chip, core = seq // 2, lax.rem(seq, 2)
    partner = {"seq": chip * 2 + 1 - core}
    pair_a = {"head": rank + 1 - 2 * lax.rem(rank, 2)}
    pair_b = {"head": 3 - rank}

    barrier = pltpu.get_barrier_semaphore()
    for turn in range(1, chips):
        other = lax.rem(chip + turn, chips)
        pl.semaphore_signal(barrier, inc=1, device_id={"seq": other * 2 + core}, device_id_type=MESH)
    for device in (partner, pair_a, pair_b):
        pl.semaphore_signal(barrier, inc=1, device_id=device, device_id_type=MESH)
    pl.semaphore_wait(barrier, chips + 2)

    side_a = lax.rem((rank + 1) // 2, 2)
    side_b = rank // 2
    plans = ((0, writes_part, pair_a, side_a, pair_b, side_b), (1, reads_part, pair_b, side_b, pair_a, side_a))

    def copy(k, step, source, target, device):
        c = pltpu.make_async_remote_copy(
            src_ref=source, dst_ref=target, send_sem=send.at[k, step], recv_sem=recv.at[k, step],
            device_id=device, device_id_type=MESH,
        )
        c.start()
        return c

    first = []
    for k, part, one, side_one, two, side_two in plans:
        give = pl.multiple_of((1 - side_one) * half, half)
        first.append(copy(k, 0, part.at[pl.ds(give, half), :], arrived.at[k, pl.ds(0, half), :], one))

    spreads = []
    for turn in range(1, chips):
        target = lax.rem(chip + turn, chips)
        c = pltpu.make_async_remote_copy(
            src_ref=block, dst_ref=blocks.at[chip], send_sem=spread_send.at[turn], recv_sem=spread_recv.at[chip],
            device_id={"seq": target * 2 + core}, device_id_type=MESH,
        )
        c.start()
        spreads.append(c)
    blocks[chip] = block[...]

    second = []
    for k, part, one, side_one, two, side_two in plans:
        first[k].wait()
        keep = pl.multiple_of(side_one * half, half)
        total[k, 0:half, :] = part[pl.ds(keep, half), :] + arrived[k, 0:half, :]
        give = pl.multiple_of((1 - side_two) * quarter, quarter)
        second.append(
            copy(k, 1, total.at[k, pl.ds(give, quarter), :], arrived.at[k, pl.ds(half, quarter), :], two)
        )
    third = []
    for k, part, one, side_one, two, side_two in plans:
        out = (writes_out, reads_out)[k]
        second[k].wait()
        keep = pl.multiple_of(side_two * quarter, quarter)
        spot = pl.ds(pl.multiple_of(side_one * half + side_two * quarter, quarter), quarter)
        out[spot, :] = total[k, pl.ds(keep, quarter), :] + arrived[k, pl.ds(half, quarter), :]
        third.append(copy(k, 2, out.at[spot, :], out.at[spot, :], two))
    fourth = []
    for k, part, one, side_one, two, side_two in plans:
        out = (writes_out, reads_out)[k]
        third[k].wait()
        spot = pl.ds(pl.multiple_of(side_one * half, half), half)
        fourth.append(copy(k, 3, out.at[spot, :], out.at[spot, :], one))

    for turn in range(1, chips):
        source = lax.rem(chip + turn, chips)
        pltpu.make_async_remote_copy(
            src_ref=block, dst_ref=blocks.at[source], send_sem=spread_send.at[turn], recv_sem=spread_recv.at[source],
            device_id={"seq": source * 2 + core}, device_id_type=MESH,
        ).wait_recv()
    near = pltpu.make_async_remote_copy(
        src_ref=blocks, dst_ref=whole.at[core], send_sem=near_send, recv_sem=near_recv,
        device_id=partner, device_id_type=MESH,
    )
    near.start()
    whole[core] = blocks[...]
    near.wait()
    for k in range(chips):
        both = jnp.concatenate([whole[0, k], whole[1, k]], axis=0)
        turned = both.T
        for e in range(2):
            for p in range(HEAD_DIM):
                initial_out[2 * k + e : 2 * k + e + 1, p * D_STATE : (p + 1) * D_STATE] = turned[
                    e * HEAD_DIM + p : e * HEAD_DIM + p + 1, :
                ]
    for c in spreads:
        c.wait_send()
    for c in fourth:
        c.wait()


def sum_part(writes_part, reads_part, block, chips):
    rows = writes_part.shape[0]
    half, quarter = rows // 2, rows // 4
    vmem = pl.BlockSpec(memory_space=pltpu.VMEM)
    dma = pltpu.SemaphoreType.DMA
    return pl.pallas_call(
        sum_kernel,
        in_specs=[vmem] * 3,
        out_specs=[vmem] * 3,
        out_shape=[
            jax.ShapeDtypeStruct((rows, D_STATE), F32),
            jax.ShapeDtypeStruct((rows, D_STATE), F32),
            jax.ShapeDtypeStruct((2 * chips, HEAD_DIM * D_STATE), F32),
        ],
        scratch_shapes=[
            pltpu.VMEM((2, half, D_STATE), F32),
            pltpu.VMEM((2, half + quarter, D_STATE), F32),
            pltpu.VMEM((chips,) + block.shape, F32),
            pltpu.VMEM((2, chips) + block.shape, F32),
            dma((2, 4)), dma((2, 4)), dma((chips,)), dma((chips,)), dma, dma,
        ],
        compiler_params=pltpu.CompilerParams(collective_id=1, has_side_effects=True, vmem_limit_bytes=VMEM_LIMIT),
        cost_estimate=pl.CostEstimate(flops=2**22, bytes_accessed=5 * 2**20, transcendentals=0),
        name="sum_part",
    )(writes_part, reads_part, block)


def per_device(chips, values, writes, reads, out_grad, log_decay, starting_head_state):
    seq = lax.axis_index("seq")
    chip, core = seq // 2, lax.rem(seq, 2)
    half = D_STATE // 2
    state, adjoint, total = local_part(values, writes, reads, out_grad, log_decay)
    start = lax.dynamic_slice(starting_head_state, (2 * chip, 0), (2, HEAD_DIM * D_STATE))
    start = start.reshape(2 * HEAD_DIM, D_STATE).T
    start = lax.dynamic_slice(start, (core * half, 0), (half, 2 * HEAD_DIM))
    entering, leaving, block = scan_part(state, adjoint, total, start, chips)
    values_grad, writes_local, reads_local = gradient_part(
        values, writes, reads, out_grad, log_decay, entering, leaving
    )
    writes_grad, reads_grad, initial_grad = sum_part(writes_local, reads_local, block, chips)
    return (values_grad, writes_grad, reads_grad, initial_grad)


def solution(mesh):
    in_specs = (
        P("seq", "head"),
        P("seq", None),
        P("seq", None),
        P("seq", "head"),
        P("head", "seq"),
        P("head", None),
    )
    out_specs = (P("seq", "head"), P("seq", None), P("seq", None), P("head", None))
    chips = mesh.shape["seq"] // 2
    return jax.shard_map(
        functools.partial(per_device, chips), mesh=mesh, in_specs=in_specs, out_specs=out_specs, check_vma=False
    )
```

```python
import functools

import jax
import jax.numpy as jnp
from jax import lax
from jax.experimental import pallas as pl
from jax.experimental.pallas import tpu as pltpu
from jax.sharding import PartitionSpec as P

HEAD_DIM = 64
D_STATE = 128
CHUNK = 128

MESH = pl.DeviceIdType.MESH
F32 = jnp.float32
BF16 = jnp.bfloat16
NN = (((1,), (0,)), ((), ()))
NT = (((1,), (1,)), ((), ()))
TN = (((0,), (0,)), ((), ()))
FUSED_LIMIT = 62 * 1024 * 1024


def dot(a, b, dims=NN):
    return lax.dot_general(a, b, dims, preferred_element_type=F32)


def split2(a):
    hi = a.astype(BF16)
    return hi, (a - hi.astype(F32)).astype(BF16)


def split3(a):
    hi = a.astype(BF16)
    rest = a - hi.astype(F32)
    mid = rest.astype(BF16)
    return hi, mid, (rest - mid.astype(F32)).astype(BF16)


def iota(shape, dim):
    return lax.broadcasted_iota(jnp.int32, shape, dim)


def spread_matrix(copies, heads):
    shape = (copies * heads, heads * HEAD_DIM)
    row = lax.rem(iota(shape, 0), heads)
    return (row == iota(shape, 1) // HEAD_DIM).astype(F32).astype(BF16)


def spread2(a, matrix):
    return dot(jnp.concatenate(split2(a), axis=1), matrix)


def fused_kernel(
    values, grads, start, writes, reads, logs,
    values_grad, writes_out, reads_out, initial_out,
    x_all, g_all, start_rows, start_block, start_turned, later, sooner, state, adjoint, total,
    near_state, near_adjoint, near_total, send_states, got_states, send_adjoints, got_adjoints,
    reply_states, came_states, reply_adjoints, came_adjoints, give_state, give_adjoint, entering, leaving,
    stacked_bf, now, scaled_hi, scaled_lo, carried, inner, ends, sums, behind, writes_part, reads_part,
    arrived, partial, block, blocks, whole,
    x_sem, g_sem, start_sem, near_send, near_recv, fs_send, fs_recv, fa_send, fa_recv,
    bs_send, bs_recv, ba_send, ba_recv, last_send, last_recv,
    sum_send, sum_recv, spread_send, spread_recv, whole_send, whole_recv, out_sem,
):
    chips = got_states.shape[0]
    half = D_STATE // 2
    lanes = 2 * HEAD_DIM
    tokens, width = x_all.shape
    heads = logs.shape[0]
    pairs = heads // 2
    size = CHUNK
    count = tokens // size
    wide = 256
    loads = tokens // wide
    seq = lax.axis_index("seq")
    rank = lax.axis_index("head")
    chip, core = seq // 2, lax.rem(seq, 2)
    is_first = core == 0
    partner = {"seq": chip * 2 + 1 - core}
    pair_a = {"head": rank + 1 - 2 * lax.rem(rank, 2)}
    pair_b = {"head": 3 - rank}
    own = pl.ds(pl.multiple_of(core * half, half), half)
    others = pl.ds(pl.multiple_of((1 - core) * half, half), half)

    def block_rows(k, n):
        return pl.ds(pl.multiple_of(k * n, n), n)

    def load(source, target, sem, k):
        rows = block_rows(k, wide)
        return pltpu.make_async_copy(source.at[rows, :], target.at[rows, :], sem.at[k])

    def remote(source, target, send, recv, device):
        return pltpu.make_async_remote_copy(
            src_ref=source, dst_ref=target, send_sem=send, recv_sem=recv, device_id=device, device_id_type=MESH
        )

    def chip_of(turn):
        return lax.rem(chip + turn, chips)

    def same_core(other):
        return {"seq": other * 2 + core}

    for k in range(loads):
        load(values, x_all, x_sem, k).start()
    for k in range(loads):
        load(grads, g_all, g_sem, k).start()
    start_copy = pltpu.make_async_copy(start.at[block_rows(chip // 4, 8), :], start_rows, start_sem)
    start_copy.start()

    barrier = pltpu.get_barrier_semaphore()
    for turn in range(1, chips):
        pl.semaphore_signal(barrier, inc=1, device_id=same_core(chip_of(turn)), device_id_type=MESH)
    for device in (partner, pair_a, pair_b):
        pl.semaphore_signal(barrier, inc=1, device_id=device, device_id_type=MESH)

    spread = spread_matrix(2, heads)

    row, col = iota((wide, wide), 0), iota((wide, wide), 1)
    after = (col > row).astype(F32).astype(BF16)
    upto_wide = (col <= row).astype(F32).astype(BF16)
    ones = jnp.ones((8, wide), BF16)
    parts = [split3(logs[:, k * wide : (k + 1) * wide]) for k in range(loads)]
    wholes = [sum(dot(ones, p, NT) for p in part) for part in parts]
    before = jnp.zeros((1, heads), F32)
    for k in range(loads):
        sooner[k * wide : (k + 1) * wide, :] = jnp.exp(sum(dot(upto_wide, p, NT) for p in parts[k]) + before)
        before = before + wholes[k][:1]
    rest = jnp.zeros((1, heads), F32)
    for k in reversed(range(loads)):
        later[k * wide : (k + 1) * wide, :] = jnp.exp(sum(dot(after, p, NT) for p in parts[k]) + rest)
        rest = rest + wholes[k][:1]
    total[...] = sum(dot(p, spread[:heads]) for p in split3(jnp.broadcast_to(before, (8, heads))))

    def local(source, target, sem, vectors, weights, result):
        def one(k, _):
            load(source, target, sem, k).wait()
            rows = block_rows(k, wide)
            hi, lo = split2(target[rows, :].astype(F32) * spread2(weights[rows, :], spread))
            v = vectors[rows, :]
            result[...] += dot(v, hi, TN) + dot(v, lo, TN)
            return 0

        return one

    state[...] = jnp.zeros_like(state)
    adjoint[...] = jnp.zeros_like(adjoint)
    lax.fori_loop(0, loads, local(values, x_all, x_sem, writes, later, state), 0)
    pl.semaphore_wait(barrier, chips + 2)
    near_total_copy = remote(total, near_total, near_send.at[0], near_recv.at[0], partner)
    near_total_copy.start()
    near_state_copy = remote(state.at[others, :], near_state, near_send.at[1], near_recv.at[1], partner)
    near_state_copy.start()
    local_adjoint = local(grads, g_all, g_sem, reads, sooner, adjoint)
    lax.fori_loop(0, loads // 2, local_adjoint, 0)

    def order(mine, near):
        return jnp.where(is_first, mine, near), jnp.where(is_first, near, mine)

    near_total_copy.wait()
    near_state_copy.wait()
    sent = []
    for turn in range(chips):
        target = chip_of(turn)
        cols = block_rows(target, lanes)
        log_first, log_second = order(total[:, cols], near_total[:, cols])
        first, second = order(state[own, cols], near_state[:, cols])
        place = got_states.at[chip] if turn == 0 else send_states.at[target]
        place[0:half, :] = jnp.exp(log_second[:1]) * first + second
        place[half:, :] = log_first + log_second
        if turn:
            copy = remote(
                send_states.at[target], got_states.at[chip], fs_send.at[turn], fs_recv.at[chip], same_core(target)
            )
            copy.start()
            sent.append(copy)
    lax.fori_loop(loads // 2, loads, local_adjoint, 0)
    near_adjoint_copy = remote(adjoint.at[others, :], near_adjoint, near_send.at[2], near_recv.at[2], partner)
    near_adjoint_copy.start()

    start_copy.wait()
    picks = [(iota((8, D_STATE), 0) == 2 * lax.rem(chip, 4) + e).astype(F32) for e in range(2)]
    for p in range(HEAD_DIM):
        lines = start_rows[:, p * D_STATE : (p + 1) * D_STATE]
        for e in range(2):
            start_block[e * HEAD_DIM + p : e * HEAD_DIM + p + 1, :] = jnp.sum(lines * picks[e], axis=0, keepdims=True)
    start_turned[...] = start_block[...].T

    now[...] = jnp.zeros_like(now)

    def forward(step, _):
        rows = block_rows(step, size)
        row, col = iota((size, size), 0), iota((size, size), 1)
        upto = (col <= row).astype(F32).astype(BF16)
        logs3 = split3(logs[:, rows])
        by_row = sum(dot(upto, p, NT) for p in logs3)
        by_col = sum(dot(p, upto, NT) for p in logs3)
        last = by_row[size - 1 :, :]
        to_end = jnp.exp(last - by_row)
        sums[step, :, :] = sum(dot(p, spread[:heads]) for p in split3(jnp.broadcast_to(last, (8, heads))))
        ends[step, :, :] = to_end
        growth = jnp.exp(sums[step, 0:1, :])
        b, c = writes[rows, :], reads[rows, :]
        x_hi, x_lo = split2(x_all[rows, :].astype(F32) * spread2(to_end, spread))
        g_hi, g_lo = split2(g_all[rows, :].astype(F32) * spread2(jnp.exp(by_row), spread))
        scaled_hi[step, :, :] = x_hi
        scaled_lo[step, :, :] = x_lo
        carried[step, :, :] = dot(jnp.concatenate([c, c], axis=0), jnp.concatenate([g_hi, g_lo], axis=0), TN)
        fresh = dot(jnp.concatenate([b, b], axis=0), jnp.concatenate([x_hi, x_lo], axis=0), TN)
        s_hi, s_lo = split2(now[...])
        outer = dot(g_hi, jnp.concatenate([s_hi, s_lo], axis=0), NT)
        outer = outer[:, :D_STATE] + outer[:, D_STATE:] + dot(g_lo, s_hi, NT)
        now[...] = growth * now[...] + fresh

        causal = col >= row
        meets = jnp.where(causal, dot(b, c, NT), 0.0)
        mixed = jnp.zeros((size, size), F32)
        low = iota((size, lanes), 1) < HEAD_DIM
        for q in range(pairs):
            cols = slice(q * lanes, (q + 1) * lanes)
            gp = g_all[rows, cols]
            zero = jnp.zeros_like(gp)
            stacked = jnp.concatenate([jnp.where(low, gp, zero), jnp.where(low, zero, gp)], axis=0)
            product = dot(x_all[rows, cols], stacked, NT)
            his, los = [], []
            for e in range(2):
                h = 2 * q + e
                decay = jnp.exp(jnp.minimum(by_col[h : h + 1, :] - by_row[:, h : h + 1], 0.0))
                mixed = mixed + product[:, e * size : (e + 1) * size] * decay
                hi, lo = split2(meets * decay)
                his.append(hi)
                los.append(lo)
            both = jnp.concatenate([jnp.concatenate(his, axis=1), jnp.concatenate(los, axis=1)], axis=0)
            both = dot(both, stacked)
            inner[step, :, cols] = both[:size] + both[size:]
        mixed = jnp.where(causal, mixed, 0.0)
        hi, lo = split2(mixed)
        writes_part[rows, :] = dot(hi, c) + dot(lo, c)
        hi, lo = split2(mixed.T)
        reads_part[rows, :] = outer + dot(hi, b) + dot(lo, b)
        return 0

    def against(hi, lo, stack):
        both = dot(hi, stack, NT)
        return both[:, :D_STATE] + both[:, D_STATE:] + dot(lo, stack[:D_STATE], NT)

    def backward(turn, _):
        k = count - 1 - turn
        rows = block_rows(k, size)
        stack = jnp.concatenate(split2(now[...]), axis=0)
        writes_part[rows, :] = writes_part[rows, :] + against(scaled_hi[k], scaled_lo[k], stack)
        b = writes[rows, :]
        outer = dot(jnp.concatenate([b, b], axis=1), stack)
        inner[k, :, :] = inner[k, :, :] + outer * spread2(ends[k], spread)
        growth = jnp.exp(sums[k, 0:1, :])
        now[...] = growth * now[...] + carried[k]
        return 0

    lax.fori_loop(0, 1, forward, 0)

    near_adjoint_copy.wait()
    for turn in range(chips):
        target = chip_of(turn)
        cols = block_rows(target, lanes)
        log_first, _ = order(total[:1, cols], near_total[:1, cols])
        first, second = order(adjoint[own, cols], near_adjoint[:, cols])
        place = got_adjoints.at[chip] if turn == 0 else send_adjoints.at[target]
        place[...] = first + jnp.exp(log_first) * second
        if turn:
            copy = remote(
                send_adjoints.at[target], got_adjoints.at[chip], fa_send.at[turn], fa_recv.at[chip], same_core(target)
            )
            copy.start()
            sent.append(copy)

    lax.fori_loop(1, 4, forward, 0)

    for turn in range(1, chips):
        source = chip_of(turn)
        remote(
            send_states.at[source], got_states.at[source], fs_send.at[turn], fs_recv.at[source], same_core(source)
        ).wait_recv()
    carry = start_turned[own, :]
    for k in range(chips):
        reply_states[k, :, :] = carry
        carry = jnp.exp(got_states[k, half : half + 1, :]) * carry + got_states[k, 0:half, :]
    for turn in range(1, chips):
        target = chip_of(turn)
        copy = remote(
            reply_states.at[target], came_states.at[chip], bs_send.at[turn], bs_recv.at[chip], same_core(target)
        )
        copy.start()
        sent.append(copy)

    lax.fori_loop(4, 7, forward, 0)

    for turn in range(1, chips):
        source = chip_of(turn)
        remote(
            send_adjoints.at[source], got_adjoints.at[source], fa_send.at[turn], fa_recv.at[source], same_core(source)
        ).wait_recv()
    carry = jnp.zeros((half, lanes), F32)
    for k in reversed(range(chips)):
        reply_adjoints[k, :, :] = carry
        carry = jnp.exp(got_states[k, half : half + 1, :]) * carry + got_adjoints[k, :, :]
    block[...] = carry
    for turn in range(1, chips):
        target = chip_of(turn)
        copy = remote(
            reply_adjoints.at[target], came_adjoints.at[chip], ba_send.at[turn], ba_recv.at[chip], same_core(target)
        )
        copy.start()
        sent.append(copy)

    lax.fori_loop(7, count, forward, 0)
    running = jnp.zeros((8, width), F32)
    for k in reversed(range(count)):
        behind[k, :, :] = jnp.exp(running)
        running = running + sums[k, :, :]
    now[...] = jnp.zeros_like(now)
    lax.fori_loop(0, count // 2, backward, 0)

    for turn in range(chips):
        source = chip_of(turn)
        if turn:
            remote(
                reply_states.at[source], came_states.at[source], bs_send.at[turn], bs_recv.at[source], same_core(source)
            ).wait_recv()
            came = came_states[source]
        else:
            came = reply_states[chip]
        cols = block_rows(source, lanes)
        log_first, _ = order(total[:1, cols], near_total[:1, cols])
        first, _ = order(state[own, cols], near_state[:, cols])
        moved = jnp.exp(log_first) * came + first
        entering[own, cols] = jnp.where(is_first, came, moved)
        give_state[:, cols] = jnp.where(is_first, moved, came)
    last_state = remote(give_state, entering.at[own, :], last_send.at[0], last_recv.at[0], partner)
    last_state.start()

    lax.fori_loop(count // 2, count, backward, 0)

    last_state.wait()
    stacked_bf[...] = jnp.concatenate(split2(entering[...]), axis=0)

    def read_incoming(k, _):
        rows = block_rows(k, wide)
        hi, lo = split2(g_all[rows, :].astype(F32) * spread2(sooner[rows, :], spread))
        reads_part[rows, :] = reads_part[rows, :] + against(hi, lo, stacked_bf[...])
        return 0

    lax.fori_loop(0, loads, read_incoming, 0)

    quarter = tokens // 4
    eighth = tokens // 8
    side_a = lax.rem((rank + 1) // 2, 2)
    side_b = rank // 2
    ways = ((pair_a, side_a, pair_b, side_b), (pair_b, side_b, pair_a, side_a))
    parts_of = (reads_part, writes_part)
    outs_of = (reads_out, writes_out)
    stages = [[None] * 8 for _ in range(2)]

    def begin(which, way, stage, source, target, device):
        index = (which * 2 + way) * 4 + stage
        copy = remote(source, target, sum_send.at[index], sum_recv.at[index], device)
        copy.start()
        stages[which][way * 4 + stage] = copy

    def advance(which, stage):
        part, out = parts_of[which], outs_of[which]
        for way, (one, side_one, two, side_two) in enumerate(ways):
            base = way * 2 * quarter
            slot = which * 2 + way
            if stage:
                stages[which][way * 4 + stage - 1].wait()
            if stage == 0:
                give = pl.multiple_of(base + (1 - side_one) * quarter, quarter)
                begin(which, way, 0, part.at[pl.ds(give, quarter), :], arrived.at[slot, pl.ds(0, quarter), :], one)
            elif stage == 1:
                keep = pl.multiple_of(base + side_one * quarter, quarter)
                partial[slot, :, :] = part[pl.ds(keep, quarter), :] + arrived[slot, 0:quarter, :]
                give = pl.multiple_of((1 - side_two) * eighth, eighth)
                begin(
                    which, way, 1, partial.at[slot, pl.ds(give, eighth), :],
                    arrived.at[slot, pl.ds(quarter, eighth), :], two,
                )
            elif stage == 2:
                keep = pl.multiple_of(side_two * eighth, eighth)
                spot = pl.ds(pl.multiple_of(base + side_one * quarter + side_two * eighth, eighth), eighth)
                out[spot, :] = partial[slot, pl.ds(keep, eighth), :] + arrived[slot, quarter : quarter + eighth, :]
                begin(which, way, 2, out.at[spot, :], out.at[spot, :], two)
            elif stage == 3:
                spot = pl.ds(pl.multiple_of(base + side_one * quarter, quarter), quarter)
                begin(which, way, 3, out.at[spot, :], out.at[spot, :], one)

    advance(0, 0)

    for turn in range(chips):
        source = chip_of(turn)
        if turn:
            remote(
                reply_adjoints.at[source], came_adjoints.at[source], ba_send.at[turn], ba_recv.at[source],
                same_core(source),
            ).wait_recv()
            came = came_adjoints[source]
        else:
            came = reply_adjoints[chip]
        cols = block_rows(source, lanes)
        _, log_second = order(total[:1, cols], near_total[:1, cols])
        _, second = order(adjoint[own, cols], near_adjoint[:, cols])
        moved = jnp.exp(log_second) * came + second
        leaving[own, cols] = jnp.where(is_first, moved, came)
        give_adjoint[:, cols] = jnp.where(is_first, came, moved)
    last_adjoint = remote(give_adjoint, leaving.at[own, :], last_send.at[1], last_recv.at[1], partner)
    last_adjoint.start()
    for turn in range(1, chips):
        target = chip_of(turn)
        copy = remote(block, blocks.at[chip], spread_send.at[turn], spread_recv.at[chip], same_core(target))
        copy.start()
        sent.append(copy)
    blocks[chip] = block[...]
    advance(0, 1)
    last_adjoint.wait()

    def write_incoming(k, _):
        rows = block_rows(k, size)
        stack = jnp.concatenate(split2(behind[k, 0:1, :] * leaving[...]), axis=0)
        writes_part[rows, :] = writes_part[rows, :] + against(scaled_hi[k], scaled_lo[k], stack)
        return 0

    def out_copy(k):
        rows = block_rows(k, size)
        return pltpu.make_async_copy(x_all.at[rows, :], values_grad.at[rows, :], out_sem.at[k])

    def value_incoming(k, _):
        rows = block_rows(k, size)
        stack = jnp.concatenate(split2(behind[k, 0:1, :] * leaving[...]), axis=0)
        b = writes[rows, :]
        outer = dot(jnp.concatenate([b, b], axis=1), stack)
        x_all[rows, :] = (inner[k, :, :] + outer * spread2(ends[k], spread)).astype(BF16)
        out_copy(k).start()
        return 0

    lax.fori_loop(0, count, write_incoming, 0)
    advance(1, 0)
    advance(0, 2)
    lax.fori_loop(0, 4, value_incoming, 0)
    advance(1, 1)
    advance(0, 3)
    lax.fori_loop(4, 6, value_incoming, 0)
    advance(1, 2)
    lax.fori_loop(6, count, value_incoming, 0)
    advance(1, 3)

    for turn in range(1, chips):
        source = chip_of(turn)
        remote(
            block, blocks.at[source], spread_send.at[turn], spread_recv.at[source], same_core(source)
        ).wait_recv()
    near_blocks = remote(blocks, whole.at[core], whole_send, whole_recv, partner)
    near_blocks.start()
    whole[core] = blocks[...]
    near_blocks.wait()
    for k in range(chips):
        turned = jnp.concatenate([whole[0, k], whole[1, k]], axis=0).T
        for e in range(2):
            for p in range(HEAD_DIM):
                initial_out[2 * k + e : 2 * k + e + 1, p * D_STATE : (p + 1) * D_STATE] = turned[
                    e * HEAD_DIM + p : e * HEAD_DIM + p + 1, :
                ]
    for copy in sent:
        copy.wait_send()
    for which in range(2):
        for way in range(2):
            stages[which][way * 4 + 3].wait()
    for k in range(count):
        out_copy(k).wait()


def fused_part(values, writes, reads, grads, logs, start, chips):
    tokens, width = values.shape
    heads = logs.shape[0]
    count = tokens // CHUNK
    loads = tokens // 256
    half = D_STATE // 2
    lanes = 2 * HEAD_DIM
    vmem = pl.BlockSpec(memory_space=pltpu.VMEM)
    hbm = pl.BlockSpec(memory_space=pl.ANY)
    dma = pltpu.SemaphoreType.DMA
    f32 = lambda *shape: pltpu.VMEM(shape, F32)
    bf16 = lambda *shape: pltpu.VMEM(shape, BF16)
    scratch = [
        bf16(tokens, width), bf16(tokens, width),
        f32(8, start.shape[1]), f32(D_STATE, lanes), f32(D_STATE, lanes),
        f32(tokens, heads), f32(tokens, heads),
        f32(D_STATE, width), f32(D_STATE, width), f32(8, width),
        f32(half, width), f32(half, width), f32(8, width),
        f32(chips, half + 8, lanes), f32(chips, half + 8, lanes),
        f32(chips, half, lanes), f32(chips, half, lanes),
        f32(chips, half, lanes), f32(chips, half, lanes),
        f32(chips, half, lanes), f32(chips, half, lanes),
        f32(half, width), f32(half, width),
        f32(D_STATE, width), f32(D_STATE, width),
        bf16(2 * D_STATE, width), f32(D_STATE, width),
        bf16(count, CHUNK, width), bf16(count, CHUNK, width),
        f32(count, D_STATE, width), f32(count, CHUNK, width),
        f32(count, CHUNK, heads), f32(count, 8, width), f32(count, 8, width),
        f32(tokens, D_STATE), f32(tokens, D_STATE),
        f32(4, tokens * 3 // 8, D_STATE), f32(4, tokens // 4, D_STATE),
        f32(half, lanes), f32(chips, half, lanes), f32(2, chips, half, lanes),
        dma((loads,)), dma((loads,)), dma, dma((3,)), dma((3,)),
        dma((chips,)), dma((chips,)), dma((chips,)), dma((chips,)),
        dma((chips,)), dma((chips,)), dma((chips,)), dma((chips,)), dma((2,)), dma((2,)),
        dma((16,)), dma((16,)), dma((chips,)), dma((chips,)), dma, dma, dma((count,)),
    ]
    return pl.pallas_call(
        fused_kernel,
        in_specs=[hbm, hbm, hbm, vmem, vmem, vmem],
        out_specs=[hbm, vmem, vmem, vmem],
        out_shape=[
            jax.ShapeDtypeStruct((tokens, width), BF16),
            jax.ShapeDtypeStruct((tokens, D_STATE), F32),
            jax.ShapeDtypeStruct((tokens, D_STATE), F32),
            jax.ShapeDtypeStruct((heads, HEAD_DIM * D_STATE), F32),
        ],
        scratch_shapes=scratch,
        compiler_params=pltpu.CompilerParams(collective_id=0, has_side_effects=True, vmem_limit_bytes=FUSED_LIMIT),
        cost_estimate=pl.CostEstimate(flops=2**34, bytes_accessed=20 * 2**20, transcendentals=0),
        name="fused_part",
    )(values, grads, start, writes, reads, logs)


def place_kernel(*refs):
    for source, target in zip(refs[:4], refs[4:]):
        target[...] = source[...]


def place_part(values_grad, writes_grad, reads_grad, initial_grad):
    tokens, width = values_grad.shape
    steps = 4
    rows = pl.BlockSpec((tokens // steps, width), lambda k: (k, 0))
    thin = pl.BlockSpec((tokens // steps, D_STATE), lambda k: (k, 0))
    cols = pl.BlockSpec((initial_grad.shape[0], initial_grad.shape[1] // steps), lambda k: (0, k))
    specs = [rows, thin, thin, cols]
    arrays = (values_grad, writes_grad, reads_grad, initial_grad)
    return pl.pallas_call(
        place_kernel,
        grid=(steps,),
        in_specs=specs,
        out_specs=specs,
        out_shape=[jax.ShapeDtypeStruct(a.shape, a.dtype) for a in arrays],
        compiler_params=pltpu.CompilerParams(vmem_limit_bytes=32 * 1024 * 1024),
        cost_estimate=pl.CostEstimate(flops=0, bytes_accessed=12 * 2**20, transcendentals=0),
        name="place_part",
    )(*arrays)


def per_device(chips, values, writes, reads, out_grad, log_decay, starting_head_state):
    return place_part(*fused_part(values, writes, reads, out_grad, log_decay, starting_head_state, chips))


def solution(mesh):
    in_specs = (
        P("seq", "head"),
        P("seq", None),
        P("seq", None),
        P("seq", "head"),
        P("head", "seq"),
        P("head", None),
    )
    out_specs = (P("seq", "head"), P("seq", None), P("seq", None), P("head", None))
    chips = mesh.shape["seq"] // 2
    return jax.shard_map(
        functools.partial(per_device, chips), mesh=mesh, in_specs=in_specs, out_specs=out_specs, check_vma=False
    )
```

```python
import functools

import jax
import jax.numpy as jnp
from jax import lax
from jax.experimental import pallas as pl
from jax.experimental.pallas import tpu as pltpu
from jax.sharding import PartitionSpec as P

HEAD_DIM = 64
D_STATE = 128
CHUNK = 128

MESH = pl.DeviceIdType.MESH
F32 = jnp.float32
BF16 = jnp.bfloat16
NN = (((1,), (0,)), ((), ()))
NT = (((1,), (1,)), ((), ()))
TN = (((0,), (0,)), ((), ()))
FUSED_LIMIT = 62 * 1024 * 1024


def dot(a, b, dims=NN):
    return lax.dot_general(a, b, dims, preferred_element_type=F32)


def split2(a):
    hi = a.astype(BF16)
    return hi, (a - hi.astype(F32)).astype(BF16)


def split3(a):
    hi = a.astype(BF16)
    rest = a - hi.astype(F32)
    mid = rest.astype(BF16)
    return hi, mid, (rest - mid.astype(F32)).astype(BF16)


def iota(shape, dim):
    return lax.broadcasted_iota(jnp.int32, shape, dim)


def spread_matrix(copies, heads):
    shape = (copies * heads, heads * HEAD_DIM)
    row = lax.rem(iota(shape, 0), heads)
    return (row == iota(shape, 1) // HEAD_DIM).astype(F32).astype(BF16)


def spread2(a, matrix):
    return dot(jnp.concatenate(split2(a), axis=1), matrix)


AHEAD = (
    (0, 0), (2, 2), (2, 1), (1, 2), (2, 3), (3, 2), (0, 2), (2, 0),
    (1, 1), (3, 3), (1, 3), (3, 1), (0, 1), (1, 0), (0, 3), (3, 0),
)


def fused_kernel(
    values, grads, start, writes, reads, logs,
    values_grad, writes_out, reads_out, initial_out,
    x_all, g_all, start_rows, start_block, start_turned, by_rows, ends, sooner, by_cols, sums, behind,
    state, adjoint, total, near_state, near_adjoint, near_total,
    send_states, got_states, send_adjoints, got_adjoints,
    reply_states, came_states, reply_adjoints, came_adjoints, give_state, give_adjoint, entering, leaving,
    entering_stack, stacks, scaled_hi, scaled_lo, inner, writes_part, reads_part,
    arrived, partial, block, blocks, whole, turned,
    x_sem, g_sem, start_sem, near_send, near_recv, fs_send, fs_recv, fa_send, fa_recv,
    bs_send, bs_recv, ba_send, ba_recv, es_send, es_recv, la_send, la_recv,
    sum_send, sum_recv, spread_send, spread_recv, whole_send, whole_recv, out_sem,
):
    chips = got_states.shape[0]
    half = D_STATE // 2
    lanes = 2 * HEAD_DIM
    tokens, width = x_all.shape
    heads = logs.shape[0]
    pairs = heads // 2
    size = CHUNK
    count = tokens // size
    wide = 256
    seq = lax.axis_index("seq")
    rank = lax.axis_index("head")
    chip, core = seq // 2, lax.rem(seq, 2)
    is_first = core == 0
    partner = {"seq": chip * 2 + 1 - core}
    pair_a = {"head": rank + 1 - 2 * lax.rem(rank, 2)}
    pair_b = {"head": 3 - rank}
    own = pl.ds(pl.multiple_of(core * half, half), half)
    others = pl.ds(pl.multiple_of((1 - core) * half, half), half)
    sent = []

    def block_rows(k, n):
        return pl.ds(pl.multiple_of(k * n, n), n)

    def load(source, target, sem, k):
        rows = block_rows(k, size)
        return pltpu.make_async_copy(source.at[rows, :], target.at[rows, :], sem.at[k])

    def remote(source, target, send, recv, device):
        return pltpu.make_async_remote_copy(
            src_ref=source, dst_ref=target, send_sem=send, recv_sem=recv, device_id=device, device_id_type=MESH
        )

    def chip_of(turn):
        dx, dz = AHEAD[turn]
        dx = dx + core * ((4 - dx) % 4 - dx)
        dz = dz + core * ((4 - dz) % 4 - dz)
        return lax.rem(chip // 4 + dx, 4) * 4 + lax.rem(chip + dz, 4)

    def same_core(other):
        return {"seq": other * 2 + core}

    def order(mine, near):
        return jnp.where(is_first, mine, near), jnp.where(is_first, near, mine)

    for k in range(count):
        load(values, x_all, x_sem, k).start()
    for k in range(count):
        load(grads, g_all, g_sem, k).start()
    start_copy = pltpu.make_async_copy(start.at[block_rows(chip // 4, 8), :], start_rows, start_sem)
    start_copy.start()

    barrier = pltpu.get_barrier_semaphore()
    for turn in range(1, chips):
        pl.semaphore_signal(barrier, inc=1, device_id=same_core(chip_of(turn)), device_id_type=MESH)
    for device in (partner, pair_a, pair_b):
        pl.semaphore_signal(barrier, inc=1, device_id=device, device_id_type=MESH)

    spread = spread_matrix(2, heads)

    row, col = iota((size, size), 0), iota((size, size), 1)
    upto = (col <= row).astype(F32).astype(BF16)
    causal = col >= row
    low = iota((size, lanes), 1) < HEAD_DIM
    before = jnp.zeros((1, heads), F32)
    for k in range(count):
        parts = split3(logs[:, k * size : (k + 1) * size])
        by_row = sum(dot(upto, p, NT) for p in parts)
        by_cols[k] = sum(dot(p, upto, NT) for p in parts)
        by_rows[k] = by_row
        last = by_row[size - 1 :, :]
        ends[k] = jnp.exp(last - by_row)
        sooner[k] = jnp.exp(before + by_row)
        sums[k] = sum(dot(p, spread[:heads]) for p in split3(jnp.broadcast_to(last, (8, heads))))
        before = before + last
    running = jnp.zeros((8, width), F32)
    for k in reversed(range(count)):
        behind[k] = jnp.exp(running)
        running = running + sums[k]
    total[...] = running

    def twice(a):
        return jnp.concatenate([a, a], axis=0)

    def against(hi, lo, stack):
        both = dot(hi, stack, NT)
        return both[:, :D_STATE] + both[:, D_STATE:] + dot(lo, stack[:D_STATE], NT)

    def ascend(k, _):
        load(values, x_all, x_sem, k).wait()
        rows = block_rows(k, size)
        hi, lo = split2(x_all[rows, :].astype(F32) * spread2(ends[k], spread))
        scaled_hi[k] = hi
        scaled_lo[k] = lo
        fresh = dot(twice(writes[rows, :]), jnp.concatenate([hi, lo], axis=0), TN)
        now = state[...]
        stacks[k] = jnp.concatenate(split2(now), axis=0)
        state[...] = jnp.exp(sums[k, 0:1, :]) * now + fresh
        return 0

    def descend(turn, _):
        k = count - 1 - turn
        load(grads, g_all, g_sem, k).wait()
        rows = block_rows(k, size)
        hi, lo = split2(g_all[rows, :].astype(F32) * spread2(jnp.exp(by_rows[k]), spread))
        carried = dot(twice(reads[rows, :]), jnp.concatenate([hi, lo], axis=0), TN)
        reads_part[rows, :] = against(hi, lo, stacks[k])
        now = adjoint[...]
        stacks[k] = jnp.concatenate(split2(now), axis=0)
        adjoint[...] = jnp.exp(sums[k, 0:1, :]) * now + carried
        return 0

    def within(k, _):
        rows = block_rows(k, size)
        by_row, by_col = by_rows[k], by_cols[k]
        b, c = writes[rows, :], reads[rows, :]
        meets = jnp.where(causal, dot(b, c, NT), 0.0)
        mixed = jnp.zeros((size, size), F32)
        for q in range(pairs):
            cols = slice(q * lanes, (q + 1) * lanes)
            gp = g_all[rows, cols]
            zero = jnp.zeros_like(gp)
            stacked = jnp.concatenate([jnp.where(low, gp, zero), jnp.where(low, zero, gp)], axis=0)
            product = dot(x_all[rows, cols], stacked, NT)
            his, los = [], []
            for e in range(2):
                h = 2 * q + e
                decay = jnp.exp(jnp.minimum(by_col[h : h + 1, :] - by_row[:, h : h + 1], 0.0))
                mixed = mixed + product[:, e * size : (e + 1) * size] * decay
                hi, lo = split2(meets * decay)
                his.append(hi)
                los.append(lo)
            both = jnp.concatenate([jnp.concatenate(his, axis=1), jnp.concatenate(los, axis=1)], axis=0)
            both = dot(both, stacked)
            inner[k, :, cols] = both[:size] + both[size:]
        mixed = jnp.where(causal, mixed, 0.0)
        hi, lo = split2(mixed)
        writes_part[rows, :] = dot(hi, c) + dot(lo, c) + against(scaled_hi[k], scaled_lo[k], stacks[k])
        hi, lo = split2(mixed.T)
        reads_part[rows, :] = reads_part[rows, :] + dot(hi, b) + dot(lo, b)
        return 0

    state[...] = jnp.zeros_like(state)
    adjoint[...] = jnp.zeros_like(adjoint)
    lax.fori_loop(0, count, ascend, 0)
    pl.semaphore_wait(barrier, chips + 2)
    near_total_copy = remote(total, near_total, near_send.at[0], near_recv.at[0], partner)
    near_total_copy.start()
    near_state_copy = remote(state.at[others, :], near_state, near_send.at[1], near_recv.at[1], partner)
    near_state_copy.start()
    lax.fori_loop(0, 3, descend, 0)

    near_total_copy.wait()
    near_state_copy.wait()
    for turn in (*range(1, chips), 0):
        target = chip_of(turn)
        cols = block_rows(target, lanes)
        log_first, log_second = order(total[:, cols], near_total[:, cols])
        first, second = order(state[own, cols], near_state[:, cols])
        place = got_states.at[chip] if turn == 0 else send_states.at[target]
        place[0:half, :] = jnp.exp(log_second[:1]) * first + second
        place[half:, :] = log_first + log_second
        if turn:
            copy = remote(
                send_states.at[target], got_states.at[chip], fs_send.at[turn], fs_recv.at[chip], same_core(target)
            )
            copy.start()
            sent.append(copy)
    lax.fori_loop(3, count, descend, 0)
    near_adjoint_copy = remote(adjoint.at[others, :], near_adjoint, near_send.at[2], near_recv.at[2], partner)
    near_adjoint_copy.start()

    start_copy.wait()
    picks = [(iota((8, D_STATE), 0) == 2 * lax.rem(chip, 4) + e).astype(F32) for e in range(2)]
    for p in range(HEAD_DIM):
        lines = start_rows[:, p * D_STATE : (p + 1) * D_STATE]
        for e in range(2):
            start_block[e * HEAD_DIM + p : e * HEAD_DIM + p + 1, :] = jnp.sum(lines * picks[e], axis=0, keepdims=True)
    start_turned[...] = start_block[...].T

    near_adjoint_copy.wait()
    for turn in (*range(1, chips), 0):
        target = chip_of(turn)
        cols = block_rows(target, lanes)
        log_first, _ = order(total[:1, cols], near_total[:1, cols])
        first, second = order(adjoint[own, cols], near_adjoint[:, cols])
        place = got_adjoints.at[chip] if turn == 0 else send_adjoints.at[target]
        place[...] = first + jnp.exp(log_first) * second
        if turn:
            copy = remote(
                send_adjoints.at[target], got_adjoints.at[chip], fa_send.at[turn], fa_recv.at[chip], same_core(target)
            )
            copy.start()
            sent.append(copy)

    lax.fori_loop(0, 2, within, 0)

    for turn in range(1, chips):
        source = chip_of(turn)
        remote(
            send_states.at[source], got_states.at[source], fs_send.at[turn], fs_recv.at[source], same_core(source)
        ).wait_recv()
    carry = start_turned[own, :]
    for k in range(chips):
        reply_states[k] = carry
        carry = jnp.exp(got_states[k, half : half + 1, :]) * carry + got_states[k, 0:half, :]
    for turn in range(1, chips):
        target = chip_of(turn)
        copy = remote(
            reply_states.at[target], came_states.at[chip], bs_send.at[turn], bs_recv.at[chip], same_core(target)
        )
        copy.start()
        sent.append(copy)

    lax.fori_loop(2, 5, within, 0)

    for turn in range(1, chips):
        source = chip_of(turn)
        remote(
            send_adjoints.at[source], got_adjoints.at[source], fa_send.at[turn], fa_recv.at[source], same_core(source)
        ).wait_recv()
    carry = jnp.zeros((half, lanes), F32)
    for k in reversed(range(chips)):
        reply_adjoints[k] = carry
        carry = jnp.exp(got_states[k, half : half + 1, :]) * carry + got_adjoints[k]
    block[...] = carry
    for turn in range(1, chips):
        target = chip_of(turn)
        copy = remote(
            reply_adjoints.at[target], came_adjoints.at[chip], ba_send.at[turn], ba_recv.at[chip], same_core(target)
        )
        copy.start()
        sent.append(copy)

    lax.fori_loop(5, count, within, 0)

    lasts = []
    for turn in range(chips):
        source = chip_of(turn)
        if turn:
            remote(
                reply_states.at[source], came_states.at[source], bs_send.at[turn], bs_recv.at[source], same_core(source)
            ).wait_recv()
            came = came_states[source]
        else:
            came = reply_states[chip]
        cols = block_rows(source, lanes)
        log_first, _ = order(total[:1, cols], near_total[:1, cols])
        first, _ = order(state[own, cols], near_state[:, cols])
        moved = jnp.exp(log_first) * came + first
        entering[own, cols] = jnp.where(is_first, came, moved)
        give_state[:, cols] = jnp.where(is_first, moved, came)
        copy = remote(give_state.at[:, cols], entering.at[own, cols], es_send.at[source], es_recv.at[source], partner)
        copy.start()
        lasts.append(copy)
    for copy in lasts:
        copy.wait()
    entering_stack[...] = jnp.concatenate(split2(entering[...]), axis=0)

    def read_incoming(k, _):
        rows = block_rows(k, size)
        hi, lo = split2(g_all[rows, :].astype(F32) * spread2(sooner[k], spread))
        reads_part[rows, :] = reads_part[rows, :] + against(hi, lo, entering_stack[...])
        return 0

    side_a = lax.rem((rank + 1) // 2, 2)
    side_b = rank // 2
    ways = ((pair_a, side_a, pair_b, side_b), (pair_b, side_b, pair_a, side_a))
    streams = [(reads_part, reads_out, way, way * 512, 512) for way in range(2)]
    streams += [(writes_part, writes_out, k % 2, k * 256, 256) for k in range(4)]
    latest = [None] * len(streams)

    def advance(stream, stage):
        part, out, way, base, rows = streams[stream]
        one, side_one, two, side_two = ways[way]
        near, far = rows // 2, rows // 4
        if stage:
            latest[stream].wait()
        if stage == 0:
            give = pl.ds(pl.multiple_of(base + (1 - side_one) * near, near), near)
            source, target, device = part.at[give, :], arrived.at[stream, pl.ds(0, near), :], one
        elif stage == 1:
            keep = pl.ds(pl.multiple_of(base + side_one * near, near), near)
            partial[stream, 0:near, :] = part[keep, :] + arrived[stream, 0:near, :]
            give = pl.ds(pl.multiple_of((1 - side_two) * far, far), far)
            source, target, device = partial.at[stream, give, :], arrived.at[stream, pl.ds(near, far), :], two
        elif stage == 2:
            keep = pl.ds(pl.multiple_of(side_two * far, far), far)
            spot = pl.ds(pl.multiple_of(base + side_one * near + side_two * far, far), far)
            out[spot, :] = partial[stream, keep, :] + arrived[stream, near : near + far, :]
            source, target, device = out.at[spot, :], out.at[spot, :], two
        elif stage == 3:
            spot = pl.ds(pl.multiple_of(base + side_one * near, near), near)
            source, target, device = out.at[spot, :], out.at[spot, :], one
        else:
            return
        index = stream * 4 + stage
        latest[stream] = remote(source, target, sum_send.at[index], sum_recv.at[index], device)
        latest[stream].start()

    lax.fori_loop(0, count // 2, read_incoming, 0)
    advance(0, 0)
    lax.fori_loop(count // 2, count, read_incoming, 0)
    advance(1, 0)

    lasts = []
    for turn in range(chips):
        source = chip_of(turn)
        if turn:
            remote(
                reply_adjoints.at[source], came_adjoints.at[source], ba_send.at[turn], ba_recv.at[source],
                same_core(source),
            ).wait_recv()
            came = came_adjoints[source]
        else:
            came = reply_adjoints[chip]
        cols = block_rows(source, lanes)
        _, log_second = order(total[:1, cols], near_total[:1, cols])
        _, second = order(adjoint[own, cols], near_adjoint[:, cols])
        moved = jnp.exp(log_second) * came + second
        leaving[own, cols] = jnp.where(is_first, moved, came)
        give_adjoint[:, cols] = jnp.where(is_first, came, moved)
        copy = remote(give_adjoint.at[:, cols], leaving.at[own, cols], la_send.at[source], la_recv.at[source], partner)
        copy.start()
        lasts.append(copy)
    for turn in range(1, chips):
        target = chip_of(turn)
        copy = remote(block, blocks.at[chip], spread_send.at[turn], spread_recv.at[chip], same_core(target))
        copy.start()
        sent.append(copy)
    blocks[chip] = block[...]
    advance(0, 1)
    advance(1, 1)
    for copy in lasts:
        copy.wait()

    def write_incoming(k, _):
        rows = block_rows(k, size)
        stack = jnp.concatenate(split2(behind[k, 0:1, :] * leaving[...]), axis=0)
        writes_part[rows, :] = writes_part[rows, :] + against(scaled_hi[k], scaled_lo[k], stack)
        return 0

    def out_copy(k):
        rows = block_rows(k, size)
        return pltpu.make_async_copy(x_all.at[rows, :], values_grad.at[rows, :], out_sem.at[k])

    def value_incoming(k, _):
        rows = block_rows(k, size)
        mine = stacks[k, 0:D_STATE, :].astype(F32) + stacks[k, D_STATE:, :].astype(F32)
        stack = jnp.concatenate(split2(mine + behind[k, 0:1, :] * leaving[...]), axis=0)
        b = writes[rows, :]
        outer = dot(jnp.concatenate([b, b], axis=1), stack)
        x_all[rows, :] = (inner[k] + outer * spread2(ends[k], spread)).astype(BF16)
        out_copy(k).start()
        return 0

    for stream in range(4):
        lax.fori_loop(2 * stream, 2 * stream + 2, write_incoming, 0)
        advance(2 + stream, 0)
        if stream == 1:
            advance(0, 2)
            advance(1, 2)

    def value_steps(first, last):
        lax.fori_loop(first, last, value_incoming, 0)

    value_steps(0, 1)
    advance(2, 1)
    advance(3, 1)
    value_steps(1, 2)
    advance(4, 1)
    advance(5, 1)
    advance(0, 3)
    advance(1, 3)
    value_steps(2, 3)
    advance(2, 2)
    advance(3, 2)
    value_steps(3, 4)
    advance(4, 2)
    advance(5, 2)

    for turn in range(1, chips):
        source = chip_of(turn)
        remote(
            block, blocks.at[source], spread_send.at[turn], spread_recv.at[source], same_core(source)
        ).wait_recv()
    near_blocks = remote(blocks, whole.at[core], whole_send, whole_recv, partner)
    near_blocks.start()
    whole[core] = blocks[...]
    value_steps(4, 5)
    advance(2, 3)
    advance(3, 3)
    value_steps(5, 6)
    advance(4, 3)
    advance(5, 3)
    value_steps(6, count)

    near_blocks.wait()
    for k in range(chips):
        turned[k * lanes : (k + 1) * lanes, :] = jnp.concatenate([whole[0, k], whole[1, k]], axis=0).T
    for first in range(0, heads, 8):
        for p in range(HEAD_DIM):
            initial_out[first : first + 8, p * D_STATE : (p + 1) * D_STATE] = turned[
                pl.ds(first * HEAD_DIM + p, 8, stride=HEAD_DIM), :
            ]
    for copy in sent:
        copy.wait_send()
    for stream in range(len(streams)):
        advance(stream, 4)
    for k in range(count):
        out_copy(k).wait()


def fused_part(values, writes, reads, grads, logs, start, chips):
    tokens, width = values.shape
    heads = logs.shape[0]
    count = tokens // CHUNK
    half = D_STATE // 2
    lanes = 2 * HEAD_DIM
    vmem = pl.BlockSpec(memory_space=pltpu.VMEM)
    hbm = pl.BlockSpec(memory_space=pl.ANY)
    dma = pltpu.SemaphoreType.DMA
    f32 = lambda *shape: pltpu.VMEM(shape, F32)
    bf16 = lambda *shape: pltpu.VMEM(shape, BF16)
    scratch = [
        bf16(tokens, width), bf16(tokens, width),
        f32(8, start.shape[1]), f32(D_STATE, lanes), f32(D_STATE, lanes),
        f32(count, CHUNK, heads), f32(count, CHUNK, heads), f32(count, CHUNK, heads),
        f32(count, heads, CHUNK), f32(count, 8, width), f32(count, 8, width),
        f32(D_STATE, width), f32(D_STATE, width), f32(8, width),
        f32(half, width), f32(half, width), f32(8, width),
        f32(chips, half + 8, lanes), f32(chips, half + 8, lanes),
        f32(chips, half, lanes), f32(chips, half, lanes),
        f32(chips, half, lanes), f32(chips, half, lanes),
        f32(chips, half, lanes), f32(chips, half, lanes),
        f32(half, width), f32(half, width),
        f32(D_STATE, width), f32(D_STATE, width),
        bf16(2 * D_STATE, width), bf16(count, 2 * D_STATE, width),
        bf16(count, CHUNK, width), bf16(count, CHUNK, width),
        f32(count, CHUNK, width),
        f32(tokens, D_STATE), f32(tokens, D_STATE),
        f32(6, 384, D_STATE), f32(6, 256, D_STATE),
        f32(half, lanes), f32(chips, half, lanes), f32(2, chips, half, lanes),
        f32(heads * HEAD_DIM, D_STATE),
        dma((count,)), dma((count,)), dma, dma((3,)), dma((3,)),
        dma((chips,)), dma((chips,)), dma((chips,)), dma((chips,)),
        dma((chips,)), dma((chips,)), dma((chips,)), dma((chips,)),
        dma((chips,)), dma((chips,)), dma((chips,)), dma((chips,)),
        dma((24,)), dma((24,)), dma((chips,)), dma((chips,)), dma, dma, dma((count,)),
    ]
    return pl.pallas_call(
        fused_kernel,
        in_specs=[hbm, hbm, hbm, vmem, vmem, vmem],
        out_specs=[hbm, vmem, vmem, vmem],
        out_shape=[
            jax.ShapeDtypeStruct((tokens, width), BF16),
            jax.ShapeDtypeStruct((tokens, D_STATE), F32),
            jax.ShapeDtypeStruct((tokens, D_STATE), F32),
            jax.ShapeDtypeStruct((heads, HEAD_DIM * D_STATE), F32),
        ],
        scratch_shapes=scratch,
        compiler_params=pltpu.CompilerParams(collective_id=0, has_side_effects=True, vmem_limit_bytes=FUSED_LIMIT),
        cost_estimate=pl.CostEstimate(flops=2**34, bytes_accessed=20 * 2**20, transcendentals=0),
        name="fused_part",
    )(values, grads, start, writes, reads, logs)


def place_kernel(*refs):
    sources, targets, sems = refs[:4], refs[4:8], refs[8]
    copies = []
    for source, target in zip(sources, targets):
        rows = source.shape[0]
        parts = 4 if source.dtype == BF16 else 1
        for k in range(parts):
            piece = pl.ds(k * (rows // parts), rows // parts)
            copies.append(pltpu.make_async_copy(source.at[piece, :], target.at[piece, :], sems.at[len(copies)]))
    for copy in copies:
        copy.start()
    for copy in copies:
        copy.wait()


def place_part(*arrays):
    hbm = pl.BlockSpec(memory_space=pl.ANY)
    return pl.pallas_call(
        place_kernel,
        in_specs=[hbm] * 4,
        out_specs=[hbm] * 4,
        out_shape=[jax.ShapeDtypeStruct(a.shape, a.dtype) for a in arrays],
        scratch_shapes=[pltpu.SemaphoreType.DMA((7,))],
        compiler_params=pltpu.CompilerParams(vmem_limit_bytes=FUSED_LIMIT),
        cost_estimate=pl.CostEstimate(flops=0, bytes_accessed=12 * 2**20, transcendentals=0),
        name="place_part",
    )(*arrays)


def per_device(chips, values, writes, reads, out_grad, log_decay, starting_head_state):
    return place_part(*fused_part(values, writes, reads, out_grad, log_decay, starting_head_state, chips))


def solution(mesh):
    in_specs = (
        P("seq", "head"),
        P("seq", None),
        P("seq", None),
        P("seq", "head"),
        P("head", "seq"),
        P("head", None),
    )
    out_specs = (P("seq", "head"), P("seq", None), P("seq", None), P("head", None))
    chips = mesh.shape["seq"] // 2
    return jax.shard_map(
        functools.partial(per_device, chips), mesh=mesh, in_specs=in_specs, out_specs=out_specs, check_vma=False
    )
```

```python
import functools

import jax
import jax.numpy as jnp
from jax import lax
from jax.experimental import pallas as pl
from jax.experimental.pallas import tpu as pltpu
from jax.sharding import PartitionSpec as P

HEAD_DIM = 64
D_STATE = 128
CHUNK = 128

MESH = pl.DeviceIdType.MESH
F32 = jnp.float32
BF16 = jnp.bfloat16
NN = (((1,), (0,)), ((), ()))
NT = (((1,), (1,)), ((), ()))
TN = (((0,), (0,)), ((), ()))
FUSED_LIMIT = 62 * 1024 * 1024


def dot(a, b, dims=NN):
    return lax.dot_general(a, b, dims, preferred_element_type=F32)


def split2(a):
    hi = a.astype(BF16)
    return hi, (a - hi.astype(F32)).astype(BF16)


def split3(a):
    hi = a.astype(BF16)
    rest = a - hi.astype(F32)
    mid = rest.astype(BF16)
    return hi, mid, (rest - mid.astype(F32)).astype(BF16)


def iota(shape, dim):
    return lax.broadcasted_iota(jnp.int32, shape, dim)


def spread_matrix(copies, heads):
    shape = (copies * heads, heads * HEAD_DIM)
    low = HEAD_DIM * (iota(shape, 0) & (heads - 1))
    col = iota(shape, 1)
    return ((col >= low) & (col < low + HEAD_DIM)).astype(F32).astype(BF16)


def spread2(a, matrix):
    return dot(jnp.concatenate(split2(a), axis=1), matrix)


AHEAD = (
    (0, 0), (2, 2), (2, 1), (1, 2), (2, 3), (3, 2), (0, 2), (2, 0),
    (1, 1), (3, 3), (1, 3), (3, 1), (0, 1), (1, 0), (0, 3), (3, 0),
)


def fused_kernel(
    values, grads, start, writes, reads, logs,
    values_grad, writes_out, reads_out, initial_out,
    x_all, g_all, start_rows, start_block, start_turned, by_rows, ends, sooner, by_cols, sums, behind,
    state, adjoint, now, total, near_state, near_adjoint, near_total,
    send_states, got_states, send_adjoints, got_adjoints,
    reply_states, came_states, reply_adjoints, came_adjoints, give_state, give_adjoint, entering, leaving,
    entering_stack, stacks, scaled_hi, scaled_lo, inner, writes_part, reads_part,
    arrived, partial, block, blocks, whole, turned,
    x_sem, g_sem, start_sem, near_send, near_recv, fs_send, fs_recv, fa_send, fa_recv,
    bs_send, bs_recv, ba_send, ba_recv, es_send, es_recv, la_send, la_recv,
    sum_send, sum_recv, spread_send, spread_recv, whole_send, whole_recv, out_sem,
):
    chips = got_states.shape[0]
    half = D_STATE // 2
    lanes = 2 * HEAD_DIM
    tokens, width = x_all.shape
    heads = logs.shape[0]
    pairs = heads // 2
    size = CHUNK
    count = tokens // size
    seq = lax.axis_index("seq")
    rank = lax.axis_index("head")
    chip, core = seq // 2, lax.rem(seq, 2)
    is_first = core == 0
    partner = {"seq": chip * 2 + 1 - core}
    pair_a = {"head": rank + 1 - 2 * lax.rem(rank, 2)}
    pair_b = {"head": 3 - rank}
    own = pl.ds(pl.multiple_of(core * half, half), half)
    others = pl.ds(pl.multiple_of((1 - core) * half, half), half)
    sent = []

    def block_rows(k, n):
        return pl.ds(pl.multiple_of(k * n, n), n)

    def load(source, target, sem, k):
        rows = block_rows(k, size)
        return pltpu.make_async_copy(source.at[rows, :], target.at[rows, :], sem.at[k])

    def remote(source, target, send, recv, device):
        return pltpu.make_async_remote_copy(
            src_ref=source, dst_ref=target, send_sem=send, recv_sem=recv, device_id=device, device_id_type=MESH
        )

    def chip_of(turn):
        dx, dz = AHEAD[turn]
        dx = dx + core * ((4 - dx) % 4 - dx)
        dz = dz + core * ((4 - dz) % 4 - dz)
        return lax.rem(chip // 4 + dx, 4) * 4 + lax.rem(chip + dz, 4)

    def same_core(other):
        return {"seq": other * 2 + core}

    def order(mine, near):
        return jnp.where(is_first, mine, near), jnp.where(is_first, near, mine)

    for k in range(count):
        load(values, x_all, x_sem, k).start()
    for k in range(count):
        load(grads, g_all, g_sem, k).start()
    start_copy = pltpu.make_async_copy(start.at[block_rows(chip // 4, 8), :], start_rows, start_sem)
    start_copy.start()

    barrier = pltpu.get_barrier_semaphore()
    for turn in range(1, chips):
        pl.semaphore_signal(barrier, inc=1, device_id=same_core(chip_of(turn)), device_id_type=MESH)
    for device in (partner, pair_a, pair_b):
        pl.semaphore_signal(barrier, inc=1, device_id=device, device_id_type=MESH)

    spread = spread_matrix(2, heads)

    row, col = iota((size, size), 0), iota((size, size), 1)
    upto = (col <= row).astype(F32).astype(BF16)
    causal = col >= row
    low = iota((size, lanes), 1) < HEAD_DIM
    parts = split3(jnp.concatenate([logs[:, k * size : (k + 1) * size] for k in range(count)], axis=0))
    by_row_all = sum(dot(upto, p, NT) for p in parts)
    by_col_all = sum(dot(p, upto, NT) for p in parts)
    before = jnp.zeros((1, heads), F32)
    lasts = []
    for k in range(count):
        by_row = by_row_all[:, k * heads : (k + 1) * heads]
        by_cols[k] = by_col_all[k * heads : (k + 1) * heads, :]
        by_rows[k] = by_row
        last = by_row[size - 1 :, :]
        ends[k] = jnp.exp(last - by_row)
        sooner[k] = jnp.exp(before + by_row)
        lasts.append(last)
        before = before + last
    sums_all = sum(dot(p, spread[:heads]) for p in split3(jnp.concatenate(lasts, axis=0)))
    running = jnp.zeros((8, width), F32)
    for k in reversed(range(count)):
        sums[k] = jnp.broadcast_to(sums_all[k : k + 1, :], (8, width))
        behind[k] = jnp.exp(running)
        running = running + sums[k]
    total[...] = running

    def twice(a):
        return jnp.concatenate([a, a], axis=0)

    def against(hi, lo, stack):
        both = dot(hi, stack, NT)
        return both[:, :D_STATE] + both[:, D_STATE:] + dot(lo, stack[:D_STATE], NT)

    def ascend(k, _):
        load(values, x_all, x_sem, k).wait()
        rows = block_rows(k, size)
        hi, lo = split2(x_all[rows, :].astype(F32) * spread2(ends[k], spread))
        scaled_hi[k] = hi
        scaled_lo[k] = lo
        fresh = dot(twice(writes[rows, :]), jnp.concatenate([hi, lo], axis=0), TN)
        state[...] = jnp.exp(sums[k, 0:1, :]) * state[...] + fresh
        return 0

    def descend(turn, _):
        k = count - 1 - turn
        load(grads, g_all, g_sem, k).wait()
        rows = block_rows(k, size)
        hi, lo = split2(g_all[rows, :].astype(F32) * spread2(jnp.exp(by_rows[k]), spread))
        carried = dot(twice(reads[rows, :]), jnp.concatenate([hi, lo], axis=0), TN)
        now = adjoint[...]
        stacks[k] = jnp.concatenate(split2(now), axis=0)
        adjoint[...] = jnp.exp(sums[k, 0:1, :]) * now + carried
        return 0

    def within(k, _):
        rows = block_rows(k, size)
        by_row, by_col = by_rows[k], by_cols[k]
        b, c = writes[rows, :], reads[rows, :]
        hi, lo = split2(g_all[rows, :].astype(F32) * spread2(jnp.exp(by_row), spread))
        reads_outer = against(hi, lo, jnp.concatenate(split2(now[...]), axis=0))
        fresh = dot(twice(b), jnp.concatenate([scaled_hi[k], scaled_lo[k]], axis=0), TN)
        now[...] = jnp.exp(sums[k, 0:1, :]) * now[...] + fresh
        meets = jnp.where(causal, dot(b, c, NT), 0.0)
        mixed = jnp.zeros((size, size), F32)
        for q in range(pairs):
            cols = slice(q * lanes, (q + 1) * lanes)
            gp = g_all[rows, cols]
            zero = jnp.zeros_like(gp)
            stacked = jnp.concatenate([jnp.where(low, gp, zero), jnp.where(low, zero, gp)], axis=0)
            product = dot(x_all[rows, cols], stacked, NT)
            his, los = [], []
            for e in range(2):
                h = 2 * q + e
                decay = jnp.exp(jnp.minimum(by_col[h : h + 1, :] - by_row[:, h : h + 1], 0.0))
                mixed = mixed + product[:, e * size : (e + 1) * size] * decay
                hi, lo = split2(meets * decay)
                his.append(hi)
                los.append(lo)
            both = jnp.concatenate([jnp.concatenate(his, axis=1), jnp.concatenate(los, axis=1)], axis=0)
            both = dot(both, stacked)
            inner[k, :, cols] = both[:size] + both[size:]
        mixed = jnp.where(causal, mixed, 0.0)
        hi, lo = split2(mixed)
        writes_part[rows, :] = dot(hi, c) + dot(lo, c) + against(scaled_hi[k], scaled_lo[k], stacks[k])
        hi, lo = split2(mixed.T)
        reads_part[rows, :] = reads_outer + dot(hi, b) + dot(lo, b)
        return 0

    now[...] = jnp.zeros_like(now)
    state[...] = jnp.zeros_like(state)
    adjoint[...] = jnp.zeros_like(adjoint)
    lax.fori_loop(0, count, ascend, 0)
    pl.semaphore_wait(barrier, chips + 2)
    near_total_copy = remote(total, near_total, near_send.at[0], near_recv.at[0], partner)
    near_total_copy.start()
    near_state_copy = remote(state.at[others, :], near_state, near_send.at[1], near_recv.at[1], partner)
    near_state_copy.start()
    lax.fori_loop(0, 3, descend, 0)

    near_total_copy.wait()
    near_state_copy.wait()
    for turn in (*range(1, chips), 0):
        target = chip_of(turn)
        cols = block_rows(target, lanes)
        log_first, log_second = order(total[:, cols], near_total[:, cols])
        first, second = order(state[own, cols], near_state[:, cols])
        place = got_states.at[chip] if turn == 0 else send_states.at[target]
        place[0:half, :] = jnp.exp(log_second[:1]) * first + second
        place[half:, :] = log_first + log_second
        if turn:
            copy = remote(
                send_states.at[target], got_states.at[chip], fs_send.at[turn], fs_recv.at[chip], same_core(target)
            )
            copy.start()
            sent.append(copy)
    lax.fori_loop(3, count, descend, 0)
    near_adjoint_copy = remote(adjoint.at[others, :], near_adjoint, near_send.at[2], near_recv.at[2], partner)
    near_adjoint_copy.start()

    start_copy.wait()
    picks = [(iota((8, D_STATE), 0) == 2 * lax.rem(chip, 4) + e).astype(F32) for e in range(2)]
    for p in range(HEAD_DIM):
        lines = start_rows[:, p * D_STATE : (p + 1) * D_STATE]
        for e in range(2):
            start_block[e * HEAD_DIM + p : e * HEAD_DIM + p + 1, :] = jnp.sum(lines * picks[e], axis=0, keepdims=True)
    start_turned[...] = start_block[...].T

    near_adjoint_copy.wait()
    for turn in (*range(1, chips), 0):
        target = chip_of(turn)
        cols = block_rows(target, lanes)
        log_first, _ = order(total[:1, cols], near_total[:1, cols])
        first, second = order(adjoint[own, cols], near_adjoint[:, cols])
        place = got_adjoints.at[chip] if turn == 0 else send_adjoints.at[target]
        place[...] = first + jnp.exp(log_first) * second
        if turn:
            copy = remote(
                send_adjoints.at[target], got_adjoints.at[chip], fa_send.at[turn], fa_recv.at[chip], same_core(target)
            )
            copy.start()
            sent.append(copy)

    lax.fori_loop(0, 2, within, 0)

    for turn in range(1, chips):
        source = chip_of(turn)
        remote(
            send_states.at[source], got_states.at[source], fs_send.at[turn], fs_recv.at[source], same_core(source)
        ).wait_recv()
    carry = start_turned[own, :]
    for k in range(chips):
        reply_states[k] = carry
        carry = jnp.exp(got_states[k, half : half + 1, :]) * carry + got_states[k, 0:half, :]
    for turn in range(1, chips):
        target = chip_of(turn)
        copy = remote(
            reply_states.at[target], came_states.at[chip], bs_send.at[turn], bs_recv.at[chip], same_core(target)
        )
        copy.start()
        sent.append(copy)

    lax.fori_loop(2, 5, within, 0)

    for turn in range(1, chips):
        source = chip_of(turn)
        remote(
            send_adjoints.at[source], got_adjoints.at[source], fa_send.at[turn], fa_recv.at[source], same_core(source)
        ).wait_recv()
    carry = jnp.zeros((half, lanes), F32)
    for k in reversed(range(chips)):
        reply_adjoints[k] = carry
        carry = jnp.exp(got_states[k, half : half + 1, :]) * carry + got_adjoints[k]
    block[...] = carry
    for turn in range(1, chips):
        target = chip_of(turn)
        copy = remote(
            reply_adjoints.at[target], came_adjoints.at[chip], ba_send.at[turn], ba_recv.at[chip], same_core(target)
        )
        copy.start()
        sent.append(copy)

    lax.fori_loop(5, count, within, 0)

    lasts = []
    for turn in range(chips):
        source = chip_of(turn)
        if turn:
            remote(
                reply_states.at[source], came_states.at[source], bs_send.at[turn], bs_recv.at[source], same_core(source)
            ).wait_recv()
            came = came_states[source]
        else:
            came = reply_states[chip]
        cols = block_rows(source, lanes)
        log_first, _ = order(total[:1, cols], near_total[:1, cols])
        first, _ = order(state[own, cols], near_state[:, cols])
        moved = jnp.exp(log_first) * came + first
        entering[own, cols] = jnp.where(is_first, came, moved)
        give_state[:, cols] = jnp.where(is_first, moved, came)
        copy = remote(give_state.at[:, cols], entering.at[own, cols], es_send.at[source], es_recv.at[source], partner)
        copy.start()
        lasts.append(copy)
    for copy in lasts:
        copy.wait()
    entering_stack[...] = jnp.concatenate(split2(entering[...]), axis=0)

    def read_incoming(k, _):
        rows = block_rows(k, size)
        hi, lo = split2(g_all[rows, :].astype(F32) * spread2(sooner[k], spread))
        reads_part[rows, :] = reads_part[rows, :] + against(hi, lo, entering_stack[...])
        return 0

    side_a = lax.rem((rank + 1) // 2, 2)
    side_b = rank // 2
    ways = ((pair_a, side_a, pair_b, side_b), (pair_b, side_b, pair_a, side_a))
    streams = [(reads_part, reads_out, way, way * 512, 512) for way in range(2)]
    streams += [(writes_part, writes_out, k % 2, k * 256, 256) for k in range(4)]
    latest = [None] * len(streams)

    def advance(stream, stage):
        part, out, way, base, rows = streams[stream]
        one, side_one, two, side_two = ways[way]
        near, far = rows // 2, rows // 4
        if stage:
            latest[stream].wait()
        if stage == 0:
            give = pl.ds(pl.multiple_of(base + (1 - side_one) * near, near), near)
            source, target, device = part.at[give, :], arrived.at[stream, pl.ds(0, near), :], one
        elif stage == 1:
            keep = pl.ds(pl.multiple_of(base + side_one * near, near), near)
            partial[stream, 0:near, :] = part[keep, :] + arrived[stream, 0:near, :]
            give = pl.ds(pl.multiple_of((1 - side_two) * far, far), far)
            source, target, device = partial.at[stream, give, :], arrived.at[stream, pl.ds(near, far), :], two
        elif stage == 2:
            keep = pl.ds(pl.multiple_of(side_two * far, far), far)
            spot = pl.ds(pl.multiple_of(base + side_one * near + side_two * far, far), far)
            out[spot, :] = partial[stream, keep, :] + arrived[stream, near : near + far, :]
            source, target, device = out.at[spot, :], out.at[spot, :], two
        elif stage == 3:
            spot = pl.ds(pl.multiple_of(base + side_one * near, near), near)
            source, target, device = out.at[spot, :], out.at[spot, :], one
        else:
            return
        index = stream * 4 + stage
        latest[stream] = remote(source, target, sum_send.at[index], sum_recv.at[index], device)
        latest[stream].start()

    lax.fori_loop(0, count // 2, read_incoming, 0)
    advance(0, 0)
    lax.fori_loop(count // 2, count, read_incoming, 0)
    advance(1, 0)

    lasts = []
    for turn in range(chips):
        source = chip_of(turn)
        if turn:
            remote(
                reply_adjoints.at[source], came_adjoints.at[source], ba_send.at[turn], ba_recv.at[source],
                same_core(source),
            ).wait_recv()
            came = came_adjoints[source]
        else:
            came = reply_adjoints[chip]
        cols = block_rows(source, lanes)
        _, log_second = order(total[:1, cols], near_total[:1, cols])
        _, second = order(adjoint[own, cols], near_adjoint[:, cols])
        moved = jnp.exp(log_second) * came + second
        leaving[own, cols] = jnp.where(is_first, moved, came)
        give_adjoint[:, cols] = jnp.where(is_first, came, moved)
        copy = remote(give_adjoint.at[:, cols], leaving.at[own, cols], la_send.at[source], la_recv.at[source], partner)
        copy.start()
        lasts.append(copy)
    for turn in range(1, chips):
        target = chip_of(turn)
        copy = remote(block, blocks.at[chip], spread_send.at[turn], spread_recv.at[chip], same_core(target))
        copy.start()
        sent.append(copy)
    blocks[chip] = block[...]
    advance(0, 1)
    advance(1, 1)
    for copy in lasts:
        copy.wait()

    def write_incoming(k, _):
        rows = block_rows(k, size)
        stack = jnp.concatenate(split2(behind[k, 0:1, :] * leaving[...]), axis=0)
        writes_part[rows, :] = writes_part[rows, :] + against(scaled_hi[k], scaled_lo[k], stack)
        return 0

    def out_copy(k):
        rows = block_rows(k, size)
        return pltpu.make_async_copy(x_all.at[rows, :], values_grad.at[rows, :], out_sem.at[k])

    def value_incoming(k, _):
        rows = block_rows(k, size)
        mine = stacks[k, 0:D_STATE, :].astype(F32) + stacks[k, D_STATE:, :].astype(F32)
        stack = jnp.concatenate(split2(mine + behind[k, 0:1, :] * leaving[...]), axis=0)
        b = writes[rows, :]
        outer = dot(jnp.concatenate([b, b], axis=1), stack)
        x_all[rows, :] = (inner[k] + outer * spread2(ends[k], spread)).astype(BF16)
        out_copy(k).start()
        return 0

    for stream in range(4):
        lax.fori_loop(2 * stream, 2 * stream + 2, write_incoming, 0)
        advance(2 + stream, 0)
        if stream == 1:
            advance(0, 2)
            advance(1, 2)

    def value_steps(first, last):
        lax.fori_loop(first, last, value_incoming, 0)

    value_steps(0, 1)
    advance(2, 1)
    advance(3, 1)
    value_steps(1, 2)
    advance(4, 1)
    advance(5, 1)
    advance(0, 3)
    advance(1, 3)
    value_steps(2, 3)
    advance(2, 2)
    advance(3, 2)
    value_steps(3, 4)
    advance(4, 2)
    advance(5, 2)

    for turn in range(1, chips):
        source = chip_of(turn)
        remote(
            block, blocks.at[source], spread_send.at[turn], spread_recv.at[source], same_core(source)
        ).wait_recv()
    near_blocks = remote(blocks, whole.at[core], whole_send, whole_recv, partner)
    near_blocks.start()
    whole[core] = blocks[...]
    value_steps(4, 5)
    advance(2, 3)
    advance(3, 3)
    value_steps(5, 6)
    advance(4, 3)
    advance(5, 3)
    value_steps(6, count)

    near_blocks.wait()
    for k in range(chips):
        turned[k * lanes : (k + 1) * lanes, :] = jnp.concatenate([whole[0, k], whole[1, k]], axis=0).T
    for first in range(0, heads, 8):
        for p in range(HEAD_DIM):
            initial_out[first : first + 8, p * D_STATE : (p + 1) * D_STATE] = turned[
                pl.ds(first * HEAD_DIM + p, 8, stride=HEAD_DIM), :
            ]
    for copy in sent:
        copy.wait_send()
    for stream in range(len(streams)):
        advance(stream, 4)
    for k in range(count):
        out_copy(k).wait()


def fused_part(values, writes, reads, grads, logs, start, chips):
    tokens, width = values.shape
    heads = logs.shape[0]
    count = tokens // CHUNK
    half = D_STATE // 2
    lanes = 2 * HEAD_DIM
    vmem = pl.BlockSpec(memory_space=pltpu.VMEM)
    hbm = pl.BlockSpec(memory_space=pl.ANY)
    dma = pltpu.SemaphoreType.DMA
    f32 = lambda *shape: pltpu.VMEM(shape, F32)
    bf16 = lambda *shape: pltpu.VMEM(shape, BF16)
    scratch = [
        bf16(tokens, width), bf16(tokens, width),
        f32(8, start.shape[1]), f32(D_STATE, lanes), f32(D_STATE, lanes),
        f32(count, CHUNK, heads), f32(count, CHUNK, heads), f32(count, CHUNK, heads),
        f32(count, heads, CHUNK), f32(count, 8, width), f32(count, 8, width),
        f32(D_STATE, width), f32(D_STATE, width), f32(D_STATE, width), f32(8, width),
        f32(half, width), f32(half, width), f32(8, width),
        f32(chips, half + 8, lanes), f32(chips, half + 8, lanes),
        f32(chips, half, lanes), f32(chips, half, lanes),
        f32(chips, half, lanes), f32(chips, half, lanes),
        f32(chips, half, lanes), f32(chips, half, lanes),
        f32(half, width), f32(half, width),
        f32(D_STATE, width), f32(D_STATE, width),
        bf16(2 * D_STATE, width), bf16(count, 2 * D_STATE, width),
        bf16(count, CHUNK, width), bf16(count, CHUNK, width),
        f32(count, CHUNK, width),
        f32(tokens, D_STATE), f32(tokens, D_STATE),
        f32(6, 384, D_STATE), f32(6, 256, D_STATE),
        f32(half, lanes), f32(chips, half, lanes), f32(2, chips, half, lanes),
        f32(heads * HEAD_DIM, D_STATE),
        dma((count,)), dma((count,)), dma, dma((3,)), dma((3,)),
        dma((chips,)), dma((chips,)), dma((chips,)), dma((chips,)),
        dma((chips,)), dma((chips,)), dma((chips,)), dma((chips,)),
        dma((chips,)), dma((chips,)), dma((chips,)), dma((chips,)),
        dma((24,)), dma((24,)), dma((chips,)), dma((chips,)), dma, dma, dma((count,)),
    ]
    return pl.pallas_call(
        fused_kernel,
        in_specs=[hbm, hbm, hbm, vmem, vmem, vmem],
        out_specs=[hbm, vmem, vmem, vmem],
        out_shape=[
            jax.ShapeDtypeStruct((tokens, width), BF16),
            jax.ShapeDtypeStruct((tokens, D_STATE), F32),
            jax.ShapeDtypeStruct((tokens, D_STATE), F32),
            jax.ShapeDtypeStruct((heads, HEAD_DIM * D_STATE), F32),
        ],
        scratch_shapes=scratch,
        compiler_params=pltpu.CompilerParams(collective_id=0, has_side_effects=True, vmem_limit_bytes=FUSED_LIMIT),
        cost_estimate=pl.CostEstimate(flops=2**34, bytes_accessed=20 * 2**20, transcendentals=0),
        name="fused_part",
    )(values, grads, start, writes, reads, logs)


def place_kernel(*refs):
    for source, target in zip(refs[:4], refs[4:]):
        target[...] = source[...]


def place_part(*arrays):
    steps = 8
    rows = [pl.BlockSpec((a.shape[0] // steps, a.shape[1]), lambda k: (k, 0)) for a in arrays[:3]]
    cols = pl.BlockSpec((arrays[3].shape[0], arrays[3].shape[1] // steps), lambda k: (0, k))
    return pl.pallas_call(
        place_kernel,
        grid=(steps,),
        in_specs=rows + [cols],
        out_specs=rows + [cols],
        out_shape=[jax.ShapeDtypeStruct(a.shape, a.dtype) for a in arrays],
        compiler_params=pltpu.CompilerParams(vmem_limit_bytes=FUSED_LIMIT),
        cost_estimate=pl.CostEstimate(flops=0, bytes_accessed=12 * 2**20, transcendentals=0),
        name="place_part",
    )(*arrays)


def per_device(chips, values, writes, reads, out_grad, log_decay, starting_head_state):
    return place_part(*fused_part(values, writes, reads, out_grad, log_decay, starting_head_state, chips))


def solution(mesh):
    in_specs = (
        P("seq", "head"),
        P("seq", None),
        P("seq", None),
        P("seq", "head"),
        P("head", "seq"),
        P("head", None),
    )
    out_specs = (P("seq", "head"), P("seq", None), P("seq", None), P("head", None))
    chips = mesh.shape["seq"] // 2
    return jax.shard_map(
        functools.partial(per_device, chips), mesh=mesh, in_specs=in_specs, out_specs=out_specs, check_vma=False
    )
```

```python
import functools

import jax
import jax.numpy as jnp
from jax import lax
from jax.experimental import pallas as pl
from jax.experimental.pallas import tpu as pltpu
from jax.sharding import PartitionSpec as P

HEAD_DIM = 64
D_STATE = 128
CHUNK = 128

MESH = pl.DeviceIdType.MESH
F32 = jnp.float32
BF16 = jnp.bfloat16
NN = (((1,), (0,)), ((), ()))
NT = (((1,), (1,)), ((), ()))
TN = (((0,), (0,)), ((), ()))
FUSED_LIMIT = 62 * 1024 * 1024


def dot(a, b, dims=NN):
    return lax.dot_general(a, b, dims, preferred_element_type=F32)


def split2(a):
    hi = a.astype(BF16)
    return hi, (a - hi.astype(F32)).astype(BF16)


def split3(a):
    hi = a.astype(BF16)
    rest = a - hi.astype(F32)
    mid = rest.astype(BF16)
    return hi, mid, (rest - mid.astype(F32)).astype(BF16)


def iota(shape, dim):
    return lax.broadcasted_iota(jnp.int32, shape, dim)


def spread_matrix(copies, heads):
    shape = (copies * heads, heads * HEAD_DIM)
    low = HEAD_DIM * (iota(shape, 0) & (heads - 1))
    col = iota(shape, 1)
    return ((col >= low) & (col < low + HEAD_DIM)).astype(F32).astype(BF16)


def spread2(a, matrix):
    return dot(jnp.concatenate(split2(a), axis=1), matrix)


AHEAD = (
    (0, 0), (2, 2), (2, 1), (1, 2), (2, 3), (3, 2), (0, 2), (2, 0),
    (1, 1), (3, 3), (1, 3), (3, 1), (0, 1), (1, 0), (0, 3), (3, 0),
)


def fused_kernel(
    values, grads, start, writes, reads, logs,
    values_grad, writes_out, reads_out, initial_out,
    x_all, g_all, start_rows, start_block, start_turned, by_rows, ends, sooner, by_cols, sums, behind,
    state, adjoint, total, near_state, near_adjoint, near_total,
    send_states, got_states, send_adjoints, got_adjoints,
    reply_states, came_states, reply_adjoints, came_adjoints, give_state, give_adjoint, entering, leaving,
    entering_stack, stacks, scaled_hi, scaled_lo, inner, writes_part, reads_part,
    arrived, partial, landed, block, blocks, whole, turned,
    x_sem, g_sem, start_sem, near_send, near_recv, fs_send, fs_recv, fa_send, fa_recv,
    bs_send, bs_recv, ba_send, ba_recv, es_send, es_recv, la_send, la_recv,
    sum_send, sum_recv, spread_send, spread_recv, whole_send, whole_recv, out_sem,
):
    chips = got_states.shape[0]
    half = D_STATE // 2
    lanes = 2 * HEAD_DIM
    tokens, width = x_all.shape
    heads = logs.shape[0]
    pairs = heads // 2
    size = CHUNK
    count = tokens // size
    seq = lax.axis_index("seq")
    rank = lax.axis_index("head")
    chip, core = seq // 2, lax.rem(seq, 2)
    is_first = core == 0
    partner = {"seq": chip * 2 + 1 - core}
    pair_a = {"head": rank + 1 - 2 * lax.rem(rank, 2)}
    pair_b = {"head": 3 - rank}
    own = pl.ds(pl.multiple_of(core * half, half), half)
    others = pl.ds(pl.multiple_of((1 - core) * half, half), half)
    sent = []

    def block_rows(k, n):
        return pl.ds(pl.multiple_of(k * n, n), n)

    def load(source, target, sem, k):
        rows = block_rows(k, size)
        return pltpu.make_async_copy(source.at[rows, :], target.at[rows, :], sem.at[k])

    def remote(source, target, send, recv, device):
        return pltpu.make_async_remote_copy(
            src_ref=source, dst_ref=target, send_sem=send, recv_sem=recv, device_id=device, device_id_type=MESH
        )

    def chip_of(turn):
        dx, dz = AHEAD[turn]
        dx = dx + core * ((4 - dx) % 4 - dx)
        dz = dz + core * ((4 - dz) % 4 - dz)
        return lax.rem(chip // 4 + dx, 4) * 4 + lax.rem(chip + dz, 4)

    def same_core(other):
        return {"seq": other * 2 + core}

    def order(mine, near):
        return jnp.where(is_first, mine, near), jnp.where(is_first, near, mine)

    for k in range(count):
        load(values, x_all, x_sem, k).start()
    for k in range(count):
        load(grads, g_all, g_sem, k).start()
    start_copy = pltpu.make_async_copy(start.at[block_rows(chip // 4, 8), :], start_rows, start_sem)
    start_copy.start()

    barrier = pltpu.get_barrier_semaphore()
    for turn in range(1, chips):
        pl.semaphore_signal(barrier, inc=1, device_id=same_core(chip_of(turn)), device_id_type=MESH)
    for device in (partner, pair_a, pair_b, {"head": lax.rem(rank + 2, 4)}):
        pl.semaphore_signal(barrier, inc=1, device_id=device, device_id_type=MESH)

    spread = spread_matrix(2, heads)

    row, col = iota((size, size), 0), iota((size, size), 1)
    upto = (col <= row).astype(F32).astype(BF16)
    causal = col >= row
    low = iota((size, lanes), 1) < HEAD_DIM
    parts = split3(jnp.concatenate([logs[:, k * size : (k + 1) * size] for k in range(count)], axis=0))
    by_row_all = sum(dot(upto, p, NT) for p in parts)
    by_col_all = sum(dot(p, upto, NT) for p in parts)
    before = jnp.zeros((1, heads), F32)
    lasts = []
    for k in range(count):
        by_row = by_row_all[:, k * heads : (k + 1) * heads]
        by_cols[k] = by_col_all[k * heads : (k + 1) * heads, :]
        by_rows[k] = by_row
        last = by_row[size - 1 :, :]
        ends[k] = jnp.exp(last - by_row)
        sooner[k] = jnp.exp(before + by_row)
        lasts.append(last)
        before = before + last
    sums_all = sum(dot(p, spread[:heads]) for p in split3(jnp.concatenate(lasts, axis=0)))
    running = jnp.zeros((8, width), F32)
    for k in reversed(range(count)):
        sums[k] = jnp.broadcast_to(sums_all[k : k + 1, :], (8, width))
        behind[k] = jnp.exp(running)
        running = running + sums[k]
    total[...] = running

    def twice(a):
        return jnp.concatenate([a, a], axis=0)

    def against(hi, lo, stack):
        both = dot(hi, stack, NT)
        return both[:, :D_STATE] + both[:, D_STATE:] + dot(lo, stack[:D_STATE], NT)

    def ascend(k, _):
        load(values, x_all, x_sem, k).wait()
        rows = block_rows(k, size)
        hi, lo = split2(x_all[rows, :].astype(F32) * spread2(ends[k], spread))
        scaled_hi[k] = hi
        scaled_lo[k] = lo
        fresh = dot(twice(writes[rows, :]), jnp.concatenate([hi, lo], axis=0), TN)
        now = state[...]
        stacks[k] = jnp.concatenate(split2(now), axis=0)
        state[...] = jnp.exp(sums[k, 0:1, :]) * now + fresh
        return 0

    def descend(turn, _):
        k = count - 1 - turn
        load(grads, g_all, g_sem, k).wait()
        rows = block_rows(k, size)
        hi, lo = split2(g_all[rows, :].astype(F32) * spread2(jnp.exp(by_rows[k]), spread))
        carried = dot(twice(reads[rows, :]), jnp.concatenate([hi, lo], axis=0), TN)
        reads_part[rows, :] = against(hi, lo, stacks[k])
        now = adjoint[...]
        stacks[k] = jnp.concatenate(split2(now), axis=0)
        adjoint[...] = jnp.exp(sums[k, 0:1, :]) * now + carried
        return 0

    def within(k, _):
        rows = block_rows(k, size)
        by_row, by_col = by_rows[k], by_cols[k]
        b, c = writes[rows, :], reads[rows, :]
        meets = jnp.where(causal, dot(b, c, NT), 0.0)
        mixed = jnp.zeros((size, size), F32)
        for q in range(pairs):
            cols = slice(q * lanes, (q + 1) * lanes)
            gp = g_all[rows, cols]
            zero = jnp.zeros_like(gp)
            stacked = jnp.concatenate([jnp.where(low, gp, zero), jnp.where(low, zero, gp)], axis=0)
            product = dot(x_all[rows, cols], stacked, NT)
            his, los = [], []
            for e in range(2):
                h = 2 * q + e
                decay = jnp.exp(jnp.minimum(by_col[h : h + 1, :] - by_row[:, h : h + 1], 0.0))
                mixed = mixed + product[:, e * size : (e + 1) * size] * decay
                hi, lo = split2(meets * decay)
                his.append(hi)
                los.append(lo)
            both = jnp.concatenate([jnp.concatenate(his, axis=1), jnp.concatenate(los, axis=1)], axis=0)
            both = dot(both, stacked)
            inner[k, :, cols] = both[:size] + both[size:]
        mixed = jnp.where(causal, mixed, 0.0)
        hi, lo = split2(mixed)
        writes_part[rows, :] = dot(hi, c) + dot(lo, c) + against(scaled_hi[k], scaled_lo[k], stacks[k])
        hi, lo = split2(mixed.T)
        reads_part[rows, :] = reads_part[rows, :] + dot(hi, b) + dot(lo, b)
        return 0

    state[...] = jnp.zeros_like(state)
    adjoint[...] = jnp.zeros_like(adjoint)
    lax.fori_loop(0, count, ascend, 0)
    pl.semaphore_wait(barrier, chips + 3)
    near_total_copy = remote(total, near_total, near_send.at[0], near_recv.at[0], partner)
    near_total_copy.start()
    near_state_copy = remote(state.at[others, :], near_state, near_send.at[1], near_recv.at[1], partner)
    near_state_copy.start()
    lax.fori_loop(0, 3, descend, 0)

    near_total_copy.wait()
    near_state_copy.wait()
    for turn in (*range(1, chips), 0):
        target = chip_of(turn)
        cols = block_rows(target, lanes)
        log_first, log_second = order(total[:, cols], near_total[:, cols])
        first, second = order(state[own, cols], near_state[:, cols])
        place = got_states.at[chip] if turn == 0 else send_states.at[target]
        place[0:half, :] = jnp.exp(log_second[:1]) * first + second
        place[half:, :] = log_first + log_second
        if turn:
            copy = remote(
                send_states.at[target], got_states.at[chip], fs_send.at[turn], fs_recv.at[chip], same_core(target)
            )
            copy.start()
            sent.append(copy)
    lax.fori_loop(3, count, descend, 0)
    near_adjoint_copy = remote(adjoint.at[others, :], near_adjoint, near_send.at[2], near_recv.at[2], partner)
    near_adjoint_copy.start()

    start_copy.wait()
    picks = [(iota((8, D_STATE), 0) == 2 * lax.rem(chip, 4) + e).astype(F32) for e in range(2)]
    for p in range(HEAD_DIM):
        lines = start_rows[:, p * D_STATE : (p + 1) * D_STATE]
        for e in range(2):
            start_block[e * HEAD_DIM + p : e * HEAD_DIM + p + 1, :] = jnp.sum(lines * picks[e], axis=0, keepdims=True)
    start_turned[...] = start_block[...].T

    near_adjoint_copy.wait()
    for turn in (*range(1, chips), 0):
        target = chip_of(turn)
        cols = block_rows(target, lanes)
        log_first, _ = order(total[:1, cols], near_total[:1, cols])
        first, second = order(adjoint[own, cols], near_adjoint[:, cols])
        place = got_adjoints.at[chip] if turn == 0 else send_adjoints.at[target]
        place[...] = first + jnp.exp(log_first) * second
        if turn:
            copy = remote(
                send_adjoints.at[target], got_adjoints.at[chip], fa_send.at[turn], fa_recv.at[chip], same_core(target)
            )
            copy.start()
            sent.append(copy)

    lax.fori_loop(0, 2, within, 0)

    for turn in range(1, chips):
        source = chip_of(turn)
        remote(
            send_states.at[source], got_states.at[source], fs_send.at[turn], fs_recv.at[source], same_core(source)
        ).wait_recv()
    carry = start_turned[own, :]
    for k in range(chips):
        reply_states[k] = carry
        carry = jnp.exp(got_states[k, half : half + 1, :]) * carry + got_states[k, 0:half, :]
    for turn in range(1, chips):
        target = chip_of(turn)
        copy = remote(
            reply_states.at[target], came_states.at[chip], bs_send.at[turn], bs_recv.at[chip], same_core(target)
        )
        copy.start()
        sent.append(copy)

    lax.fori_loop(2, 5, within, 0)

    for turn in range(1, chips):
        source = chip_of(turn)
        remote(
            send_adjoints.at[source], got_adjoints.at[source], fa_send.at[turn], fa_recv.at[source], same_core(source)
        ).wait_recv()
    carry = jnp.zeros((half, lanes), F32)
    for k in reversed(range(chips)):
        reply_adjoints[k] = carry
        carry = jnp.exp(got_states[k, half : half + 1, :]) * carry + got_adjoints[k]
    block[...] = carry
    for turn in range(1, chips):
        target = chip_of(turn)
        copy = remote(
            reply_adjoints.at[target], came_adjoints.at[chip], ba_send.at[turn], ba_recv.at[chip], same_core(target)
        )
        copy.start()
        sent.append(copy)

    lax.fori_loop(5, count, within, 0)

    lasts = []
    for turn in range(chips):
        source = chip_of(turn)
        if turn:
            remote(
                reply_states.at[source], came_states.at[source], bs_send.at[turn], bs_recv.at[source], same_core(source)
            ).wait_recv()
            came = came_states[source]
        else:
            came = reply_states[chip]
        cols = block_rows(source, lanes)
        log_first, _ = order(total[:1, cols], near_total[:1, cols])
        first, _ = order(state[own, cols], near_state[:, cols])
        moved = jnp.exp(log_first) * came + first
        entering[own, cols] = jnp.where(is_first, came, moved)
        give_state[:, cols] = jnp.where(is_first, moved, came)
        copy = remote(give_state.at[:, cols], entering.at[own, cols], es_send.at[source], es_recv.at[source], partner)
        copy.start()
        lasts.append(copy)
    for copy in lasts:
        copy.wait()
    entering_stack[...] = jnp.concatenate(split2(entering[...]), axis=0)

    def read_incoming(k, _):
        rows = block_rows(k, size)
        hi, lo = split2(g_all[rows, :].astype(F32) * spread2(sooner[k], spread))
        reads_part[rows, :] = reads_part[rows, :] + against(hi, lo, entering_stack[...])
        return 0

    side_a = lax.rem((rank + 1) // 2, 2)
    side_b = rank // 2
    ways = ((pair_a, side_a, pair_b, side_b), (pair_b, side_b, pair_a, side_a))
    streams = [(reads_part, reads_out, way, way * 512, 512) for way in range(2)]
    latest = [None] * len(streams)

    def advance(stream, stage):
        part, out, way, base, rows = streams[stream]
        one, side_one, two, side_two = ways[way]
        near, far = rows // 2, rows // 4
        if stage:
            latest[stream].wait()
        if stage == 0:
            give = pl.ds(pl.multiple_of(base + (1 - side_one) * near, near), near)
            source, target, device = part.at[give, :], arrived.at[stream, pl.ds(0, near), :], one
        elif stage == 1:
            keep = pl.ds(pl.multiple_of(base + side_one * near, near), near)
            partial[stream, 0:near, :] = part[keep, :] + arrived[stream, 0:near, :]
            give = pl.ds(pl.multiple_of((1 - side_two) * far, far), far)
            source, target, device = partial.at[stream, give, :], arrived.at[stream, pl.ds(near, far), :], two
        elif stage == 2:
            keep = pl.ds(pl.multiple_of(side_two * far, far), far)
            spot = pl.ds(pl.multiple_of(base + side_one * near + side_two * far, far), far)
            out[spot, :] = partial[stream, keep, :] + arrived[stream, near : near + far, :]
            source, target, device = out.at[spot, :], out.at[spot, :], two
        elif stage == 3:
            spot = pl.ds(pl.multiple_of(base + side_one * near, near), near)
            source, target, device = out.at[spot, :], out.at[spot, :], one
        else:
            return
        index = stream * 4 + stage
        latest[stream] = remote(source, target, sum_send.at[index], sum_recv.at[index], device)
        latest[stream].start()

    piece = tokens // 16

    def piece_rows(stream, owner):
        return pl.ds(pl.multiple_of(stream * 4 * piece + owner * piece, piece), piece)

    def direct(stream, step, stage):
        other = lax.rem(rank + step, 4)
        index = 8 + stream * 6 + stage * 3 + step - 1
        if stage == 0:
            source, target = writes_part.at[piece_rows(stream, other), :], landed.at[stream, step - 1]
        else:
            source = target = writes_out.at[piece_rows(stream, rank), :]
        return remote(source, target, sum_send.at[index], sum_recv.at[index], {"head": other})

    def scatter(stream):
        for step in (2, 1, 3):
            direct(stream, step, 0).start()

    def gather(stream):
        for step in (2, 1, 3):
            direct(stream, step, 0).wait()
        rows = piece_rows(stream, rank)
        writes_out[rows, :] = (writes_part[rows, :] + landed[stream, 0]) + (landed[stream, 1] + landed[stream, 2])
        for step in (2, 1, 3):
            direct(stream, step, 1).start()

    lax.fori_loop(0, count // 2, read_incoming, 0)
    advance(0, 0)
    lax.fori_loop(count // 2, count, read_incoming, 0)
    advance(1, 0)

    lasts = []
    for turn in range(chips):
        source = chip_of(turn)
        if turn:
            remote(
                reply_adjoints.at[source], came_adjoints.at[source], ba_send.at[turn], ba_recv.at[source],
                same_core(source),
            ).wait_recv()
            came = came_adjoints[source]
        else:
            came = reply_adjoints[chip]
        cols = block_rows(source, lanes)
        _, log_second = order(total[:1, cols], near_total[:1, cols])
        _, second = order(adjoint[own, cols], near_adjoint[:, cols])
        moved = jnp.exp(log_second) * came + second
        leaving[own, cols] = jnp.where(is_first, moved, came)
        give_adjoint[:, cols] = jnp.where(is_first, came, moved)
        copy = remote(give_adjoint.at[:, cols], leaving.at[own, cols], la_send.at[source], la_recv.at[source], partner)
        copy.start()
        lasts.append(copy)
    for turn in range(1, chips):
        target = chip_of(turn)
        copy = remote(block, blocks.at[chip], spread_send.at[turn], spread_recv.at[chip], same_core(target))
        copy.start()
        sent.append(copy)
    blocks[chip] = block[...]
    advance(0, 1)
    advance(1, 1)
    for copy in lasts:
        copy.wait()

    def write_incoming(k, _):
        rows = block_rows(k, size)
        stack = jnp.concatenate(split2(behind[k, 0:1, :] * leaving[...]), axis=0)
        writes_part[rows, :] = writes_part[rows, :] + against(scaled_hi[k], scaled_lo[k], stack)
        return 0

    def out_copy(k):
        rows = block_rows(k, size)
        return pltpu.make_async_copy(x_all.at[rows, :], values_grad.at[rows, :], out_sem.at[k])

    def value_incoming(k, _):
        rows = block_rows(k, size)
        mine = stacks[k, 0:D_STATE, :].astype(F32) + stacks[k, D_STATE:, :].astype(F32)
        stack = jnp.concatenate(split2(mine + behind[k, 0:1, :] * leaving[...]), axis=0)
        b = writes[rows, :]
        outer = dot(jnp.concatenate([b, b], axis=1), stack)
        x_all[rows, :] = (inner[k] + outer * spread2(ends[k], spread)).astype(BF16)
        out_copy(k).start()
        return 0

    for stream in range(4):
        lax.fori_loop(2 * stream, 2 * stream + 2, write_incoming, 0)
        scatter(stream)
        if stream == 1:
            advance(0, 2)
            advance(1, 2)

    def value_steps(first, last):
        lax.fori_loop(first, last, value_incoming, 0)

    gather(0)
    value_steps(0, 1)
    gather(1)
    value_steps(1, 2)
    gather(2)
    advance(0, 3)
    advance(1, 3)
    value_steps(2, 3)
    gather(3)
    value_steps(3, 4)

    for turn in range(1, chips):
        source = chip_of(turn)
        remote(
            block, blocks.at[source], spread_send.at[turn], spread_recv.at[source], same_core(source)
        ).wait_recv()
    near_blocks = remote(blocks, whole.at[core], whole_send, whole_recv, partner)
    near_blocks.start()
    whole[core] = blocks[...]
    value_steps(4, count)

    near_blocks.wait()
    for k in range(chips):
        turned[k * lanes : (k + 1) * lanes, :] = jnp.concatenate([whole[0, k], whole[1, k]], axis=0).T
    for first in range(0, heads, 8):
        for p in range(HEAD_DIM):
            initial_out[first : first + 8, p * D_STATE : (p + 1) * D_STATE] = turned[
                pl.ds(first * HEAD_DIM + p, 8, stride=HEAD_DIM), :
            ]
    for copy in sent:
        copy.wait_send()
    for stream in range(len(streams)):
        advance(stream, 4)
    for stream in range(4):
        for step in range(1, 4):
            direct(stream, step, 1).wait()
    for k in range(count):
        out_copy(k).wait()


def fused_part(values, writes, reads, grads, logs, start, chips):
    tokens, width = values.shape
    heads = logs.shape[0]
    count = tokens // CHUNK
    half = D_STATE // 2
    lanes = 2 * HEAD_DIM
    vmem = pl.BlockSpec(memory_space=pltpu.VMEM)
    hbm = pl.BlockSpec(memory_space=pl.ANY)
    dma = pltpu.SemaphoreType.DMA
    f32 = lambda *shape: pltpu.VMEM(shape, F32)
    bf16 = lambda *shape: pltpu.VMEM(shape, BF16)
    scratch = [
        bf16(tokens, width), bf16(tokens, width),
        f32(8, start.shape[1]), f32(D_STATE, lanes), f32(D_STATE, lanes),
        f32(count, CHUNK, heads), f32(count, CHUNK, heads), f32(count, CHUNK, heads),
        f32(count, heads, CHUNK), f32(count, 8, width), f32(count, 8, width),
        f32(D_STATE, width), f32(D_STATE, width), f32(8, width),
        f32(half, width), f32(half, width), f32(8, width),
        f32(chips, half + 8, lanes), f32(chips, half + 8, lanes),
        f32(chips, half, lanes), f32(chips, half, lanes),
        f32(chips, half, lanes), f32(chips, half, lanes),
        f32(chips, half, lanes), f32(chips, half, lanes),
        f32(half, width), f32(half, width),
        f32(D_STATE, width), f32(D_STATE, width),
        bf16(2 * D_STATE, width), bf16(count, 2 * D_STATE, width),
        bf16(count, CHUNK, width), bf16(count, CHUNK, width),
        f32(count, CHUNK, width),
        f32(tokens, D_STATE), f32(tokens, D_STATE),
        f32(2, 384, D_STATE), f32(2, 256, D_STATE), f32(4, 3, tokens // 16, D_STATE),
        f32(half, lanes), f32(chips, half, lanes), f32(2, chips, half, lanes),
        f32(heads * HEAD_DIM, D_STATE),
        dma((count,)), dma((count,)), dma, dma((3,)), dma((3,)),
        dma((chips,)), dma((chips,)), dma((chips,)), dma((chips,)),
        dma((chips,)), dma((chips,)), dma((chips,)), dma((chips,)),
        dma((chips,)), dma((chips,)), dma((chips,)), dma((chips,)),
        dma((32,)), dma((32,)), dma((chips,)), dma((chips,)), dma, dma, dma((count,)),
    ]
    return pl.pallas_call(
        fused_kernel,
        in_specs=[hbm, hbm, hbm, vmem, vmem, vmem],
        out_specs=[hbm, vmem, vmem, vmem],
        out_shape=[
            jax.ShapeDtypeStruct((tokens, width), BF16),
            jax.ShapeDtypeStruct((tokens, D_STATE), F32),
            jax.ShapeDtypeStruct((tokens, D_STATE), F32),
            jax.ShapeDtypeStruct((heads, HEAD_DIM * D_STATE), F32),
        ],
        scratch_shapes=scratch,
        compiler_params=pltpu.CompilerParams(collective_id=0, has_side_effects=True, vmem_limit_bytes=FUSED_LIMIT),
        cost_estimate=pl.CostEstimate(flops=2**34, bytes_accessed=20 * 2**20, transcendentals=0),
        name="fused_part",
    )(values, grads, start, writes, reads, logs)


PIECES = (8, 1, 1, 2)


def place_kernel(*refs):
    sources, targets, holds, in_sem, out_sem = refs[:4], refs[4:8], refs[8:12], refs[12], refs[13]
    ins, outs = [], []
    for source, target, hold, pieces in zip(sources, targets, holds, PIECES):
        rows = source.shape[0] // pieces
        for k in range(pieces):
            piece = pl.ds(k * rows, rows)
            ins.append(pltpu.make_async_copy(source.at[piece, :], hold.at[piece, :], in_sem.at[len(ins)]))
            outs.append(pltpu.make_async_copy(hold.at[piece, :], target.at[piece, :], out_sem.at[len(outs)]))
    for copy in ins:
        copy.start()
    for came, goes in zip(ins, outs):
        came.wait()
        goes.start()
    for copy in outs:
        copy.wait()


def place_part(*arrays):
    hbm = pl.BlockSpec(memory_space=pl.ANY)
    sems = pltpu.SemaphoreType.DMA((sum(PIECES),))
    return pl.pallas_call(
        place_kernel,
        in_specs=[hbm] * 4,
        out_specs=[hbm] * 4,
        out_shape=[jax.ShapeDtypeStruct(a.shape, a.dtype) for a in arrays],
        scratch_shapes=[pltpu.VMEM(a.shape, a.dtype) for a in arrays] + [sems, sems],
        compiler_params=pltpu.CompilerParams(vmem_limit_bytes=FUSED_LIMIT),
        cost_estimate=pl.CostEstimate(flops=0, bytes_accessed=12 * 2**20, transcendentals=0),
        name="place_part",
    )(*arrays)


def per_device(chips, values, writes, reads, out_grad, log_decay, starting_head_state):
    return place_part(*fused_part(values, writes, reads, out_grad, log_decay, starting_head_state, chips))


def solution(mesh):
    in_specs = (
        P("seq", "head"),
        P("seq", None),
        P("seq", None),
        P("seq", "head"),
        P("head", "seq"),
        P("head", None),
    )
    out_specs = (P("seq", "head"), P("seq", None), P("seq", None), P("head", None))
    chips = mesh.shape["seq"] // 2
    return jax.shard_map(
        functools.partial(per_device, chips), mesh=mesh, in_specs=in_specs, out_specs=out_specs, check_vma=False
    )
```

```python
import functools

import jax
import jax.numpy as jnp
from jax import lax
from jax.experimental import pallas as pl
from jax.experimental.pallas import tpu as pltpu
from jax.sharding import PartitionSpec as P

HEAD_DIM = 64
D_STATE = 128
CHUNK = 128

MESH = pl.DeviceIdType.MESH
F32 = jnp.float32
BF16 = jnp.bfloat16
NN = (((1,), (0,)), ((), ()))
NT = (((1,), (1,)), ((), ()))
TN = (((0,), (0,)), ((), ()))
FUSED_LIMIT = 62 * 1024 * 1024


def dot(a, b, dims=NN):
    return lax.dot_general(a, b, dims, preferred_element_type=F32)


def split2(a):
    hi = a.astype(BF16)
    return hi, (a - hi.astype(F32)).astype(BF16)


def split3(a):
    hi = a.astype(BF16)
    rest = a - hi.astype(F32)
    mid = rest.astype(BF16)
    return hi, mid, (rest - mid.astype(F32)).astype(BF16)


def iota(shape, dim):
    return lax.broadcasted_iota(jnp.int32, shape, dim)


def spread_matrix(copies, heads):
    shape = (copies * heads, heads * HEAD_DIM)
    low = HEAD_DIM * (iota(shape, 0) & (heads - 1))
    col = iota(shape, 1)
    return ((col >= low) & (col < low + HEAD_DIM)).astype(F32).astype(BF16)


def spread2(a, matrix):
    return dot(jnp.concatenate(split2(a), axis=1), matrix)


AHEAD = (
    (0, 0), (2, 2), (2, 1), (1, 2), (2, 3), (3, 2), (0, 2), (2, 0),
    (1, 1), (3, 3), (1, 3), (3, 1), (0, 1), (1, 0), (0, 3), (3, 0),
)


def fused_kernel(
    values, grads, start, writes, reads, logs,
    values_grad, writes_out, reads_out, initial_out,
    x_all, g_all, start_rows, start_block, start_turned, by_rows, ends, sooner, by_cols, sums, behind,
    state, adjoint, total, near_state, near_adjoint, near_total,
    send_states, got_states, send_adjoints, got_adjoints,
    reply_states, came_states, reply_adjoints, came_adjoints, give_state, give_adjoint, entering, leaving,
    entering_stack, stacks, scaled_hi, scaled_lo, inner, writes_part, reads_part,
    landed, block, blocks, whole, turned,
    x_sem, g_sem, start_sem, near_send, near_recv, fs_send, fs_recv, fa_send, fa_recv,
    bs_send, bs_recv, ba_send, ba_recv, es_send, es_recv, la_send, la_recv,
    sum_send, sum_recv, spread_send, spread_recv, whole_send, whole_recv, out_sem,
):
    chips = got_states.shape[0]
    half = D_STATE // 2
    lanes = 2 * HEAD_DIM
    tokens, width = x_all.shape
    heads = logs.shape[0]
    pairs = heads // 2
    size = CHUNK
    count = tokens // size
    seq = lax.axis_index("seq")
    rank = lax.axis_index("head")
    chip, core = seq // 2, lax.rem(seq, 2)
    is_first = core == 0
    partner = {"seq": chip * 2 + 1 - core}
    own = pl.ds(pl.multiple_of(core * half, half), half)
    others = pl.ds(pl.multiple_of((1 - core) * half, half), half)
    sent = []

    def block_rows(k, n):
        return pl.ds(pl.multiple_of(k * n, n), n)

    def load(source, target, sem, k):
        rows = block_rows(k, size)
        return pltpu.make_async_copy(source.at[rows, :], target.at[rows, :], sem.at[k])

    def remote(source, target, send, recv, device):
        return pltpu.make_async_remote_copy(
            src_ref=source, dst_ref=target, send_sem=send, recv_sem=recv, device_id=device, device_id_type=MESH
        )

    def chip_of(turn):
        dx, dz = AHEAD[turn]
        dx = dx + core * ((4 - dx) % 4 - dx)
        dz = dz + core * ((4 - dz) % 4 - dz)
        return lax.rem(chip // 4 + dx, 4) * 4 + lax.rem(chip + dz, 4)

    def same_core(other):
        return {"seq": other * 2 + core}

    def order(mine, near):
        return jnp.where(is_first, mine, near), jnp.where(is_first, near, mine)

    for k in range(count):
        load(values, x_all, x_sem, k).start()
    for k in range(count):
        load(grads, g_all, g_sem, k).start()
    start_copy = pltpu.make_async_copy(start.at[block_rows(chip // 4, 8), :], start_rows, start_sem)
    start_copy.start()

    barrier = pltpu.get_barrier_semaphore()
    for turn in range(1, chips):
        pl.semaphore_signal(barrier, inc=1, device_id=same_core(chip_of(turn)), device_id_type=MESH)
    for device in (partner, *({"head": lax.rem(rank + step, 4)} for step in (1, 2, 3))):
        pl.semaphore_signal(barrier, inc=1, device_id=device, device_id_type=MESH)

    spread = spread_matrix(2, heads)

    row, col = iota((size, size), 0), iota((size, size), 1)
    upto = (col <= row).astype(F32).astype(BF16)
    causal = col >= row
    low = iota((size, lanes), 1) < HEAD_DIM
    parts = split3(jnp.concatenate([logs[:, k * size : (k + 1) * size] for k in range(count)], axis=0))
    by_row_all = sum(dot(upto, p, NT) for p in parts)
    by_col_all = sum(dot(p, upto, NT) for p in parts)
    before = jnp.zeros((1, heads), F32)
    lasts = []
    for k in range(count):
        by_row = by_row_all[:, k * heads : (k + 1) * heads]
        by_cols[k] = by_col_all[k * heads : (k + 1) * heads, :]
        by_rows[k] = by_row
        last = by_row[size - 1 :, :]
        ends[k] = jnp.exp(last - by_row)
        sooner[k] = jnp.exp(before + by_row)
        lasts.append(last)
        before = before + last
    sums_all = sum(dot(p, spread[:heads]) for p in split3(jnp.concatenate(lasts, axis=0)))
    running = jnp.zeros((8, width), F32)
    for k in reversed(range(count)):
        sums[k] = jnp.broadcast_to(sums_all[k : k + 1, :], (8, width))
        behind[k] = jnp.exp(running)
        running = running + sums[k]
    total[...] = running

    def twice(a):
        return jnp.concatenate([a, a], axis=0)

    def against(hi, lo, stack):
        both = dot(hi, stack, NT)
        return both[:, :D_STATE] + both[:, D_STATE:] + dot(lo, stack[:D_STATE], NT)

    def ascend(k, _):
        load(values, x_all, x_sem, k).wait()
        rows = block_rows(k, size)
        hi, lo = split2(x_all[rows, :].astype(F32) * spread2(ends[k], spread))
        scaled_hi[k] = hi
        scaled_lo[k] = lo
        fresh = dot(twice(writes[rows, :]), jnp.concatenate([hi, lo], axis=0), TN)
        now = state[...]
        stacks[k] = jnp.concatenate(split2(now), axis=0)
        state[...] = jnp.exp(sums[k, 0:1, :]) * now + fresh
        return 0

    def descend(turn, _):
        k = count - 1 - turn
        load(grads, g_all, g_sem, k).wait()
        rows = block_rows(k, size)
        hi, lo = split2(g_all[rows, :].astype(F32) * spread2(jnp.exp(by_rows[k]), spread))
        carried = dot(twice(reads[rows, :]), jnp.concatenate([hi, lo], axis=0), TN)
        reads_part[rows, :] = against(hi, lo, stacks[k])
        now = adjoint[...]
        stacks[k] = jnp.concatenate(split2(now), axis=0)
        adjoint[...] = jnp.exp(sums[k, 0:1, :]) * now + carried
        return 0

    def within(k, _):
        rows = block_rows(k, size)
        by_row, by_col = by_rows[k], by_cols[k]
        b, c = writes[rows, :], reads[rows, :]
        meets = jnp.where(causal, dot(b, c, NT), 0.0)
        mixed = jnp.zeros((size, size), F32)
        for q in range(pairs):
            cols = slice(q * lanes, (q + 1) * lanes)
            gp = g_all[rows, cols]
            zero = jnp.zeros_like(gp)
            stacked = jnp.concatenate([jnp.where(low, gp, zero), jnp.where(low, zero, gp)], axis=0)
            product = dot(x_all[rows, cols], stacked, NT)
            his, los = [], []
            for e in range(2):
                h = 2 * q + e
                decay = jnp.exp(jnp.minimum(by_col[h : h + 1, :] - by_row[:, h : h + 1], 0.0))
                mixed = mixed + product[:, e * size : (e + 1) * size] * decay
                hi, lo = split2(meets * decay)
                his.append(hi)
                los.append(lo)
            both = jnp.concatenate([jnp.concatenate(his, axis=1), jnp.concatenate(los, axis=1)], axis=0)
            both = dot(both, stacked)
            inner[k, :, cols] = both[:size] + both[size:]
        mixed = jnp.where(causal, mixed, 0.0)
        hi, lo = split2(mixed)
        writes_part[rows, :] = dot(hi, c) + dot(lo, c) + against(scaled_hi[k], scaled_lo[k], stacks[k])
        hi, lo = split2(mixed.T)
        reads_part[rows, :] = reads_part[rows, :] + dot(hi, b) + dot(lo, b)
        return 0

    state[...] = jnp.zeros_like(state)
    adjoint[...] = jnp.zeros_like(adjoint)
    lax.fori_loop(0, count, ascend, 0)
    pl.semaphore_wait(barrier, chips + 3)
    near_total_copy = remote(total, near_total, near_send.at[0], near_recv.at[0], partner)
    near_total_copy.start()
    near_state_copy = remote(state.at[others, :], near_state, near_send.at[1], near_recv.at[1], partner)
    near_state_copy.start()
    lax.fori_loop(0, 3, descend, 0)

    near_total_copy.wait()
    near_state_copy.wait()
    for turn in (*range(1, chips), 0):
        target = chip_of(turn)
        cols = block_rows(target, lanes)
        log_first, log_second = order(total[:, cols], near_total[:, cols])
        first, second = order(state[own, cols], near_state[:, cols])
        place = got_states.at[chip] if turn == 0 else send_states.at[target]
        place[0:half, :] = jnp.exp(log_second[:1]) * first + second
        place[half:, :] = log_first + log_second
        if turn:
            copy = remote(
                send_states.at[target], got_states.at[chip], fs_send.at[turn], fs_recv.at[chip], same_core(target)
            )
            copy.start()
            sent.append(copy)
    lax.fori_loop(3, count, descend, 0)
    near_adjoint_copy = remote(adjoint.at[others, :], near_adjoint, near_send.at[2], near_recv.at[2], partner)
    near_adjoint_copy.start()

    start_copy.wait()
    picks = [(iota((8, D_STATE), 0) == 2 * lax.rem(chip, 4) + e).astype(F32) for e in range(2)]
    for p in range(HEAD_DIM):
        lines = start_rows[:, p * D_STATE : (p + 1) * D_STATE]
        for e in range(2):
            start_block[e * HEAD_DIM + p : e * HEAD_DIM + p + 1, :] = jnp.sum(lines * picks[e], axis=0, keepdims=True)
    start_turned[...] = start_block[...].T

    near_adjoint_copy.wait()
    for turn in (*range(1, chips), 0):
        target = chip_of(turn)
        cols = block_rows(target, lanes)
        log_first, _ = order(total[:1, cols], near_total[:1, cols])
        first, second = order(adjoint[own, cols], near_adjoint[:, cols])
        place = got_adjoints.at[chip] if turn == 0 else send_adjoints.at[target]
        place[...] = first + jnp.exp(log_first) * second
        if turn:
            copy = remote(
                send_adjoints.at[target], got_adjoints.at[chip], fa_send.at[turn], fa_recv.at[chip], same_core(target)
            )
            copy.start()
            sent.append(copy)

    lax.fori_loop(0, 2, within, 0)

    for turn in range(1, chips):
        source = chip_of(turn)
        remote(
            send_states.at[source], got_states.at[source], fs_send.at[turn], fs_recv.at[source], same_core(source)
        ).wait_recv()
    carry = start_turned[own, :]
    for k in range(chips):
        reply_states[k] = carry
        carry = jnp.exp(got_states[k, half : half + 1, :]) * carry + got_states[k, 0:half, :]
    for turn in range(1, chips):
        target = chip_of(turn)
        copy = remote(
            reply_states.at[target], came_states.at[chip], bs_send.at[turn], bs_recv.at[chip], same_core(target)
        )
        copy.start()
        sent.append(copy)

    lax.fori_loop(2, 5, within, 0)

    for turn in range(1, chips):
        source = chip_of(turn)
        remote(
            send_adjoints.at[source], got_adjoints.at[source], fa_send.at[turn], fa_recv.at[source], same_core(source)
        ).wait_recv()
    carry = jnp.zeros((half, lanes), F32)
    for k in reversed(range(chips)):
        reply_adjoints[k] = carry
        carry = jnp.exp(got_states[k, half : half + 1, :]) * carry + got_adjoints[k]
    block[...] = carry
    for turn in range(1, chips):
        target = chip_of(turn)
        copy = remote(
            reply_adjoints.at[target], came_adjoints.at[chip], ba_send.at[turn], ba_recv.at[chip], same_core(target)
        )
        copy.start()
        sent.append(copy)

    lax.fori_loop(5, count, within, 0)

    lasts = []
    for turn in range(chips):
        source = chip_of(turn)
        if turn:
            remote(
                reply_states.at[source], came_states.at[source], bs_send.at[turn], bs_recv.at[source], same_core(source)
            ).wait_recv()
            came = came_states[source]
        else:
            came = reply_states[chip]
        cols = block_rows(source, lanes)
        log_first, _ = order(total[:1, cols], near_total[:1, cols])
        first, _ = order(state[own, cols], near_state[:, cols])
        moved = jnp.exp(log_first) * came + first
        entering[own, cols] = jnp.where(is_first, came, moved)
        give_state[:, cols] = jnp.where(is_first, moved, came)
        copy = remote(give_state.at[:, cols], entering.at[own, cols], es_send.at[source], es_recv.at[source], partner)
        copy.start()
        lasts.append(copy)
    for copy in lasts:
        copy.wait()
    entering_stack[...] = jnp.concatenate(split2(entering[...]), axis=0)

    def read_incoming(k, _):
        rows = block_rows(k, size)
        hi, lo = split2(g_all[rows, :].astype(F32) * spread2(sooner[k], spread))
        reads_part[rows, :] = reads_part[rows, :] + against(hi, lo, entering_stack[...])
        return 0

    piece = tokens // 16

    sides = ((reads_part, reads_out), (writes_part, writes_out))

    def piece_rows(stream, owner):
        return pl.ds(pl.multiple_of((stream % 4) * 4 * piece + owner * piece, piece), piece)

    def direct(stream, step, stage):
        other = lax.rem(rank + step, 4)
        part, out = sides[stream // 4]
        index = stream * 6 + stage * 3 + step - 1
        if stage == 0:
            source, target = part.at[piece_rows(stream, other), :], landed.at[stream, step - 1]
        else:
            source = target = out.at[piece_rows(stream, rank), :]
        return remote(source, target, sum_send.at[index], sum_recv.at[index], {"head": other})

    def scatter(stream):
        for step in (2, 1, 3):
            direct(stream, step, 0).start()

    def gather(stream):
        for step in (2, 1, 3):
            direct(stream, step, 0).wait()
        rows = piece_rows(stream, rank)
        part, out = sides[stream // 4]
        out[rows, :] = (part[rows, :] + landed[stream, 0]) + (landed[stream, 1] + landed[stream, 2])
        for step in (2, 1, 3):
            direct(stream, step, 1).start()

    for stream in range(4):
        lax.fori_loop(2 * stream, 2 * stream + 2, read_incoming, 0)
        scatter(stream)

    lasts = []
    for turn in range(chips):
        source = chip_of(turn)
        if turn:
            remote(
                reply_adjoints.at[source], came_adjoints.at[source], ba_send.at[turn], ba_recv.at[source],
                same_core(source),
            ).wait_recv()
            came = came_adjoints[source]
        else:
            came = reply_adjoints[chip]
        cols = block_rows(source, lanes)
        _, log_second = order(total[:1, cols], near_total[:1, cols])
        _, second = order(adjoint[own, cols], near_adjoint[:, cols])
        moved = jnp.exp(log_second) * came + second
        leaving[own, cols] = jnp.where(is_first, moved, came)
        give_adjoint[:, cols] = jnp.where(is_first, came, moved)
        copy = remote(give_adjoint.at[:, cols], leaving.at[own, cols], la_send.at[source], la_recv.at[source], partner)
        copy.start()
        lasts.append(copy)
    for turn in range(1, chips):
        target = chip_of(turn)
        copy = remote(block, blocks.at[chip], spread_send.at[turn], spread_recv.at[chip], same_core(target))
        copy.start()
        sent.append(copy)
    blocks[chip] = block[...]
    for stream in range(4):
        gather(stream)
    for copy in lasts:
        copy.wait()

    def write_incoming(k, _):
        rows = block_rows(k, size)
        stack = jnp.concatenate(split2(behind[k, 0:1, :] * leaving[...]), axis=0)
        writes_part[rows, :] = writes_part[rows, :] + against(scaled_hi[k], scaled_lo[k], stack)
        return 0

    def out_copy(k):
        rows = block_rows(k, size)
        return pltpu.make_async_copy(x_all.at[rows, :], values_grad.at[rows, :], out_sem.at[k])

    def value_incoming(k, _):
        rows = block_rows(k, size)
        mine = stacks[k, 0:D_STATE, :].astype(F32) + stacks[k, D_STATE:, :].astype(F32)
        stack = jnp.concatenate(split2(mine + behind[k, 0:1, :] * leaving[...]), axis=0)
        b = writes[rows, :]
        outer = dot(jnp.concatenate([b, b], axis=1), stack)
        x_all[rows, :] = (inner[k] + outer * spread2(ends[k], spread)).astype(BF16)
        out_copy(k).start()
        return 0

    for stream in range(4):
        lax.fori_loop(2 * stream, 2 * stream + 2, write_incoming, 0)
        scatter(4 + stream)

    def value_steps(first, last):
        lax.fori_loop(first, last, value_incoming, 0)

    gather(4)
    value_steps(0, 1)
    gather(5)
    value_steps(1, 2)
    gather(6)
    value_steps(2, 3)
    gather(7)
    value_steps(3, 4)

    for turn in range(1, chips):
        source = chip_of(turn)
        remote(
            block, blocks.at[source], spread_send.at[turn], spread_recv.at[source], same_core(source)
        ).wait_recv()
    near_blocks = remote(blocks, whole.at[core], whole_send, whole_recv, partner)
    near_blocks.start()
    whole[core] = blocks[...]
    value_steps(4, count)

    near_blocks.wait()
    for k in range(chips):
        turned[k * lanes : (k + 1) * lanes, :] = jnp.concatenate([whole[0, k], whole[1, k]], axis=0).T
    for first in range(0, heads, 8):
        for p in range(HEAD_DIM):
            initial_out[first : first + 8, p * D_STATE : (p + 1) * D_STATE] = turned[
                pl.ds(first * HEAD_DIM + p, 8, stride=HEAD_DIM), :
            ]
    for copy in sent:
        copy.wait_send()
    for stream in range(8):
        for step in range(1, 4):
            direct(stream, step, 1).wait()
    for k in range(count):
        out_copy(k).wait()


def fused_part(values, writes, reads, grads, logs, start, chips):
    tokens, width = values.shape
    heads = logs.shape[0]
    count = tokens // CHUNK
    half = D_STATE // 2
    lanes = 2 * HEAD_DIM
    vmem = pl.BlockSpec(memory_space=pltpu.VMEM)
    hbm = pl.BlockSpec(memory_space=pl.ANY)
    dma = pltpu.SemaphoreType.DMA
    f32 = lambda *shape: pltpu.VMEM(shape, F32)
    bf16 = lambda *shape: pltpu.VMEM(shape, BF16)
    scratch = [
        bf16(tokens, width), bf16(tokens, width),
        f32(8, start.shape[1]), f32(D_STATE, lanes), f32(D_STATE, lanes),
        f32(count, CHUNK, heads), f32(count, CHUNK, heads), f32(count, CHUNK, heads),
        f32(count, heads, CHUNK), f32(count, 8, width), f32(count, 8, width),
        f32(D_STATE, width), f32(D_STATE, width), f32(8, width),
        f32(half, width), f32(half, width), f32(8, width),
        f32(chips, half + 8, lanes), f32(chips, half + 8, lanes),
        f32(chips, half, lanes), f32(chips, half, lanes),
        f32(chips, half, lanes), f32(chips, half, lanes),
        f32(chips, half, lanes), f32(chips, half, lanes),
        f32(half, width), f32(half, width),
        f32(D_STATE, width), f32(D_STATE, width),
        bf16(2 * D_STATE, width), bf16(count, 2 * D_STATE, width),
        bf16(count, CHUNK, width), bf16(count, CHUNK, width),
        f32(count, CHUNK, width),
        f32(tokens, D_STATE), f32(tokens, D_STATE),
        f32(8, 3, tokens // 16, D_STATE),
        f32(half, lanes), f32(chips, half, lanes), f32(2, chips, half, lanes),
        f32(heads * HEAD_DIM, D_STATE),
        dma((count,)), dma((count,)), dma, dma((3,)), dma((3,)),
        dma((chips,)), dma((chips,)), dma((chips,)), dma((chips,)),
        dma((chips,)), dma((chips,)), dma((chips,)), dma((chips,)),
        dma((chips,)), dma((chips,)), dma((chips,)), dma((chips,)),
        dma((48,)), dma((48,)), dma((chips,)), dma((chips,)), dma, dma, dma((count,)),
    ]
    return pl.pallas_call(
        fused_kernel,
        in_specs=[hbm, hbm, hbm, vmem, vmem, vmem],
        out_specs=[hbm, vmem, vmem, vmem],
        out_shape=[
            jax.ShapeDtypeStruct((tokens, width), BF16),
            jax.ShapeDtypeStruct((tokens, D_STATE), F32),
            jax.ShapeDtypeStruct((tokens, D_STATE), F32),
            jax.ShapeDtypeStruct((heads, HEAD_DIM * D_STATE), F32),
        ],
        scratch_shapes=scratch,
        compiler_params=pltpu.CompilerParams(collective_id=0, has_side_effects=True, vmem_limit_bytes=FUSED_LIMIT),
        cost_estimate=pl.CostEstimate(flops=2**34, bytes_accessed=20 * 2**20, transcendentals=0),
        name="fused_part",
    )(values, grads, start, writes, reads, logs)


PIECES = (8, 1, 1, 2)


def place_kernel(*refs):
    sources, targets, holds, in_sem, out_sem = refs[:4], refs[4:8], refs[8:12], refs[12], refs[13]
    ins, outs = [], []
    for source, target, hold, pieces in zip(sources, targets, holds, PIECES):
        rows = source.shape[0] // pieces
        for k in range(pieces):
            piece = pl.ds(k * rows, rows)
            ins.append(pltpu.make_async_copy(source.at[piece, :], hold.at[piece, :], in_sem.at[len(ins)]))
            outs.append(pltpu.make_async_copy(hold.at[piece, :], target.at[piece, :], out_sem.at[len(outs)]))
    for copy in ins:
        copy.start()
    for came, goes in zip(ins, outs):
        came.wait()
        goes.start()
    for copy in outs:
        copy.wait()


def place_part(*arrays):
    hbm = pl.BlockSpec(memory_space=pl.ANY)
    sems = pltpu.SemaphoreType.DMA((sum(PIECES),))
    return pl.pallas_call(
        place_kernel,
        in_specs=[hbm] * 4,
        out_specs=[hbm] * 4,
        out_shape=[jax.ShapeDtypeStruct(a.shape, a.dtype) for a in arrays],
        scratch_shapes=[pltpu.VMEM(a.shape, a.dtype) for a in arrays] + [sems, sems],
        compiler_params=pltpu.CompilerParams(vmem_limit_bytes=FUSED_LIMIT),
        cost_estimate=pl.CostEstimate(flops=0, bytes_accessed=12 * 2**20, transcendentals=0),
        name="place_part",
    )(*arrays)


def per_device(chips, values, writes, reads, out_grad, log_decay, starting_head_state):
    return place_part(*fused_part(values, writes, reads, out_grad, log_decay, starting_head_state, chips))


def solution(mesh):
    in_specs = (
        P("seq", "head"),
        P("seq", None),
        P("seq", None),
        P("seq", "head"),
        P("head", "seq"),
        P("head", None),
    )
    out_specs = (P("seq", "head"), P("seq", None), P("seq", None), P("head", None))
    chips = mesh.shape["seq"] // 2
    return jax.shard_map(
        functools.partial(per_device, chips), mesh=mesh, in_specs=in_specs, out_specs=out_specs, check_vma=False
    )
```

```python
import functools

import jax
import jax.numpy as jnp
from jax import lax
from jax.experimental import pallas as pl
from jax.experimental.pallas import tpu as pltpu
from jax.sharding import PartitionSpec as P

HEAD_DIM = 64
D_STATE = 128
CHUNK = 128

MESH = pl.DeviceIdType.MESH
F32 = jnp.float32
BF16 = jnp.bfloat16
NN = (((1,), (0,)), ((), ()))
NT = (((1,), (1,)), ((), ()))
TN = (((0,), (0,)), ((), ()))
FUSED_LIMIT = 62 * 1024 * 1024


def dot(a, b, dims=NN):
    return lax.dot_general(a, b, dims, preferred_element_type=F32)


def split2(a):
    hi = a.astype(BF16)
    return hi, (a - hi.astype(F32)).astype(BF16)


def split3(a):
    hi = a.astype(BF16)
    rest = a - hi.astype(F32)
    mid = rest.astype(BF16)
    return hi, mid, (rest - mid.astype(F32)).astype(BF16)


def iota(shape, dim):
    return lax.broadcasted_iota(jnp.int32, shape, dim)


def spread_matrix(copies, heads):
    shape = (copies * heads, heads * HEAD_DIM)
    low = HEAD_DIM * (iota(shape, 0) & (heads - 1))
    col = iota(shape, 1)
    return ((col >= low) & (col < low + HEAD_DIM)).astype(F32).astype(BF16)


def spread2(a, matrix):
    return dot(jnp.concatenate(split2(a), axis=1), matrix)


AHEAD = (
    (0, 0), (2, 2), (2, 1), (1, 2), (2, 3), (3, 2), (0, 2), (2, 0),
    (1, 1), (3, 3), (1, 3), (3, 1), (0, 1), (1, 0), (0, 3), (3, 0),
)


def fused_kernel(
    values, grads, start, writes, reads, logs,
    values_grad, writes_out, reads_out, initial_out,
    x_all, g_all, start_rows, start_block, start_turned, by_rows, ends, sooner, by_cols, sums, behind,
    state, adjoint, total, near_state, near_adjoint, near_total,
    send_states, got_states, send_adjoints, got_adjoints,
    reply_states, came_states, reply_adjoints, came_adjoints, give_state, give_adjoint, entering, leaving,
    entering_stack, stacks, scaled_hi, scaled_lo, inner, writes_part, reads_part,
    landed, block, blocks, whole, turned,
    x_sem, g_sem, start_sem, near_send, near_recv, fs_send, fs_recv, fa_send, fa_recv,
    bs_send, bs_recv, ba_send, ba_recv, es_send, es_recv, la_send, la_recv,
    sum_send, sum_recv, spread_send, spread_recv, whole_send, whole_recv, out_sem,
):
    chips = got_states.shape[0]
    half = D_STATE // 2
    lanes = 2 * HEAD_DIM
    tokens, width = x_all.shape
    heads = logs.shape[0]
    pairs = heads // 2
    size = CHUNK
    count = tokens // size
    seq = lax.axis_index("seq")
    rank = lax.axis_index("head")
    chip, core = seq // 2, lax.rem(seq, 2)
    is_first = core == 0
    partner = {"seq": chip * 2 + 1 - core}
    own = pl.ds(pl.multiple_of(core * half, half), half)
    others = pl.ds(pl.multiple_of((1 - core) * half, half), half)
    sent = []

    def block_rows(k, n):
        return pl.ds(pl.multiple_of(k * n, n), n)

    def load(source, target, sem, k):
        rows = block_rows(k, size)
        return pltpu.make_async_copy(source.at[rows, :], target.at[rows, :], sem.at[k])

    def remote(source, target, send, recv, device):
        return pltpu.make_async_remote_copy(
            src_ref=source, dst_ref=target, send_sem=send, recv_sem=recv, device_id=device, device_id_type=MESH
        )

    def chip_of(turn):
        dx, dz = AHEAD[turn]
        dx = dx + core * ((4 - dx) % 4 - dx)
        dz = dz + core * ((4 - dz) % 4 - dz)
        return lax.rem(chip // 4 + dx, 4) * 4 + lax.rem(chip + dz, 4)

    def same_core(other):
        return {"seq": other * 2 + core}

    def order(mine, near):
        return jnp.where(is_first, mine, near), jnp.where(is_first, near, mine)

    for k in range(count):
        load(values, x_all, x_sem, k).start()
    for k in range(count):
        load(grads, g_all, g_sem, k).start()
    start_copy = pltpu.make_async_copy(start.at[block_rows(chip // 4, 8), :], start_rows, start_sem)
    start_copy.start()

    barrier = pltpu.get_barrier_semaphore()
    for turn in range(1, chips):
        pl.semaphore_signal(barrier, inc=1, device_id=same_core(chip_of(turn)), device_id_type=MESH)
    for device in (partner, *({"head": lax.rem(rank + step, 4)} for step in (1, 2, 3))):
        pl.semaphore_signal(barrier, inc=1, device_id=device, device_id_type=MESH)

    spread = spread_matrix(2, heads)

    row, col = iota((size, size), 0), iota((size, size), 1)
    upto = (col <= row).astype(F32).astype(BF16)
    causal = col >= row
    low = iota((size, lanes), 1) < HEAD_DIM
    parts = split3(jnp.concatenate([logs[:, k * size : (k + 1) * size] for k in range(count)], axis=0))
    by_row_all = sum(dot(upto, p, NT) for p in parts)
    by_col_all = sum(dot(p, upto, NT) for p in parts)
    before = jnp.zeros((1, heads), F32)
    lasts = []
    for k in range(count):
        by_row = by_row_all[:, k * heads : (k + 1) * heads]
        by_cols[k] = by_col_all[k * heads : (k + 1) * heads, :]
        by_rows[k] = by_row
        last = by_row[size - 1 :, :]
        ends[k] = jnp.exp(last - by_row)
        sooner[k] = jnp.exp(before + by_row)
        lasts.append(last)
        before = before + last
    sums_all = sum(dot(p, spread[:heads]) for p in split3(jnp.concatenate(lasts, axis=0)))
    running = jnp.zeros((8, width), F32)
    for k in reversed(range(count)):
        sums[k] = jnp.broadcast_to(sums_all[k : k + 1, :], (8, width))
        behind[k] = jnp.exp(running)
        running = running + sums[k]
    total[...] = running

    def twice(a):
        return jnp.concatenate([a, a], axis=0)

    def against(hi, lo, stack):
        both = dot(hi, stack, NT)
        return both[:, :D_STATE] + both[:, D_STATE:] + dot(lo, stack[:D_STATE], NT)

    def ascend(k, _):
        load(values, x_all, x_sem, k).wait()
        rows = block_rows(k, size)
        hi, lo = split2(x_all[rows, :].astype(F32) * spread2(ends[k], spread))
        scaled_hi[k] = hi
        scaled_lo[k] = lo
        fresh = dot(twice(writes[rows, :]), jnp.concatenate([hi, lo], axis=0), TN)
        now = state[...]
        stacks[k] = jnp.concatenate(split2(now), axis=0)
        state[...] = jnp.exp(sums[k, 0:1, :]) * now + fresh
        return 0

    def descend(turn, _):
        k = count - 1 - turn
        load(grads, g_all, g_sem, k).wait()
        rows = block_rows(k, size)
        hi, lo = split2(g_all[rows, :].astype(F32) * spread2(jnp.exp(by_rows[k]), spread))
        carried = dot(twice(reads[rows, :]), jnp.concatenate([hi, lo], axis=0), TN)
        reads_part[rows, :] = against(hi, lo, stacks[k])
        now = adjoint[...]
        stacks[k] = jnp.concatenate(split2(now), axis=0)
        adjoint[...] = jnp.exp(sums[k, 0:1, :]) * now + carried
        return 0

    def within(k, _):
        rows = block_rows(k, size)
        by_row, by_col = by_rows[k], by_cols[k]
        b, c = writes[rows, :], reads[rows, :]
        meets = jnp.where(causal, dot(b, c, NT), 0.0)
        mixed = jnp.zeros((size, size), F32)
        for q in range(pairs):
            cols = slice(q * lanes, (q + 1) * lanes)
            gp = g_all[rows, cols]
            zero = jnp.zeros_like(gp)
            stacked = jnp.concatenate([jnp.where(low, gp, zero), jnp.where(low, zero, gp)], axis=0)
            product = dot(x_all[rows, cols], stacked, NT)
            his, los = [], []
            for e in range(2):
                h = 2 * q + e
                decay = jnp.exp(jnp.minimum(by_col[h : h + 1, :] - by_row[:, h : h + 1], 0.0))
                mixed = mixed + product[:, e * size : (e + 1) * size] * decay
                hi, lo = split2(meets * decay)
                his.append(hi)
                los.append(lo)
            both = jnp.concatenate([jnp.concatenate(his, axis=1), jnp.concatenate(los, axis=1)], axis=0)
            both = dot(both, stacked)
            inner[k, :, cols] = both[:size] + both[size:]
        mixed = jnp.where(causal, mixed, 0.0)
        hi, lo = split2(mixed)
        writes_part[rows, :] = dot(hi, c) + dot(lo, c) + against(scaled_hi[k], scaled_lo[k], stacks[k])
        hi, lo = split2(mixed.T)
        reads_part[rows, :] = reads_part[rows, :] + dot(hi, b) + dot(lo, b)
        return 0

    state[...] = jnp.zeros_like(state)
    adjoint[...] = jnp.zeros_like(adjoint)
    lax.fori_loop(0, count, ascend, 0, unroll=2)
    pl.semaphore_wait(barrier, chips + 3)
    near_total_copy = remote(total, near_total, near_send.at[0], near_recv.at[0], partner)
    near_total_copy.start()
    near_state_copy = remote(state.at[others, :], near_state, near_send.at[1], near_recv.at[1], partner)
    near_state_copy.start()
    lax.fori_loop(0, 2, descend, 0, unroll=2)

    near_total_copy.wait()
    near_state_copy.wait()
    for turn in (*range(1, chips), 0):
        target = chip_of(turn)
        cols = block_rows(target, lanes)
        log_first, log_second = order(total[:, cols], near_total[:, cols])
        first, second = order(state[own, cols], near_state[:, cols])
        place = got_states.at[chip] if turn == 0 else send_states.at[target]
        place[0:half, :] = jnp.exp(log_second[:1]) * first + second
        place[half:, :] = log_first + log_second
        if turn:
            copy = remote(
                send_states.at[target], got_states.at[chip], fs_send.at[turn], fs_recv.at[chip], same_core(target)
            )
            copy.start()
            sent.append(copy)
    lax.fori_loop(2, count, descend, 0, unroll=2)
    near_adjoint_copy = remote(adjoint.at[others, :], near_adjoint, near_send.at[2], near_recv.at[2], partner)
    near_adjoint_copy.start()

    start_copy.wait()
    picks = [(iota((8, D_STATE), 0) == 2 * lax.rem(chip, 4) + e).astype(F32) for e in range(2)]
    for p in range(HEAD_DIM):
        lines = start_rows[:, p * D_STATE : (p + 1) * D_STATE]
        for e in range(2):
            start_block[e * HEAD_DIM + p : e * HEAD_DIM + p + 1, :] = jnp.sum(lines * picks[e], axis=0, keepdims=True)
    start_turned[...] = start_block[...].T

    near_adjoint_copy.wait()
    for turn in (*range(1, chips), 0):
        target = chip_of(turn)
        cols = block_rows(target, lanes)
        log_first, _ = order(total[:1, cols], near_total[:1, cols])
        first, second = order(adjoint[own, cols], near_adjoint[:, cols])
        place = got_adjoints.at[chip] if turn == 0 else send_adjoints.at[target]
        place[...] = first + jnp.exp(log_first) * second
        if turn:
            copy = remote(
                send_adjoints.at[target], got_adjoints.at[chip], fa_send.at[turn], fa_recv.at[chip], same_core(target)
            )
            copy.start()
            sent.append(copy)

    lax.fori_loop(0, 2, within, 0)

    for turn in range(1, chips):
        source = chip_of(turn)
        remote(
            send_states.at[source], got_states.at[source], fs_send.at[turn], fs_recv.at[source], same_core(source)
        ).wait_recv()
    carry = start_turned[own, :]
    for k in range(chips):
        reply_states[k] = carry
        carry = jnp.exp(got_states[k, half : half + 1, :]) * carry + got_states[k, 0:half, :]
    for turn in range(1, chips):
        target = chip_of(turn)
        copy = remote(
            reply_states.at[target], came_states.at[chip], bs_send.at[turn], bs_recv.at[chip], same_core(target)
        )
        copy.start()
        sent.append(copy)

    lax.fori_loop(2, 5, within, 0)

    for turn in range(1, chips):
        source = chip_of(turn)
        remote(
            send_adjoints.at[source], got_adjoints.at[source], fa_send.at[turn], fa_recv.at[source], same_core(source)
        ).wait_recv()
    carry = jnp.zeros((half, lanes), F32)
    for k in reversed(range(chips)):
        reply_adjoints[k] = carry
        carry = jnp.exp(got_states[k, half : half + 1, :]) * carry + got_adjoints[k]
    block[...] = carry
    for turn in range(1, chips):
        target = chip_of(turn)
        copy = remote(
            reply_adjoints.at[target], came_adjoints.at[chip], ba_send.at[turn], ba_recv.at[chip], same_core(target)
        )
        copy.start()
        sent.append(copy)

    lax.fori_loop(5, count, within, 0)

    lasts = []
    for turn in range(chips):
        source = chip_of(turn)
        if turn:
            remote(
                reply_states.at[source], came_states.at[source], bs_send.at[turn], bs_recv.at[source], same_core(source)
            ).wait_recv()
            came = came_states[source]
        else:
            came = reply_states[chip]
        cols = block_rows(source, lanes)
        log_first, _ = order(total[:1, cols], near_total[:1, cols])
        first, _ = order(state[own, cols], near_state[:, cols])
        moved = jnp.exp(log_first) * came + first
        entering[own, cols] = jnp.where(is_first, came, moved)
        give_state[:, cols] = jnp.where(is_first, moved, came)
        copy = remote(give_state.at[:, cols], entering.at[own, cols], es_send.at[source], es_recv.at[source], partner)
        copy.start()
        lasts.append(copy)
    for copy in lasts:
        copy.wait()
    entering_stack[...] = jnp.concatenate(split2(entering[...]), axis=0)

    def read_incoming(k, _):
        rows = block_rows(k, size)
        hi, lo = split2(g_all[rows, :].astype(F32) * spread2(sooner[k], spread))
        reads_part[rows, :] = reads_part[rows, :] + against(hi, lo, entering_stack[...])
        return 0

    piece = tokens // 16

    sides = ((reads_part, reads_out), (writes_part, writes_out))

    def piece_rows(stream, owner):
        return pl.ds(pl.multiple_of((stream % 4) * 4 * piece + owner * piece, piece), piece)

    def direct(stream, step, stage):
        other = lax.rem(rank + step, 4)
        part, out = sides[stream // 4]
        index = stream * 6 + stage * 3 + step - 1
        if stage == 0:
            source, target = part.at[piece_rows(stream, other), :], landed.at[stream, step - 1]
        else:
            source = target = out.at[piece_rows(stream, rank), :]
        return remote(source, target, sum_send.at[index], sum_recv.at[index], {"head": other})

    def scatter(stream):
        for step in (2, 1, 3):
            direct(stream, step, 0).start()

    def gather(stream):
        for step in (2, 1, 3):
            direct(stream, step, 0).wait()
        rows = piece_rows(stream, rank)
        part, out = sides[stream // 4]
        out[rows, :] = (part[rows, :] + landed[stream, 0]) + (landed[stream, 1] + landed[stream, 2])
        for step in (2, 1, 3):
            direct(stream, step, 1).start()

    for stream in range(4):
        lax.fori_loop(2 * stream, 2 * stream + 2, read_incoming, 0, unroll=2)
        scatter(stream)

    lasts = []
    for turn in range(chips):
        source = chip_of(turn)
        if turn:
            remote(
                reply_adjoints.at[source], came_adjoints.at[source], ba_send.at[turn], ba_recv.at[source],
                same_core(source),
            ).wait_recv()
            came = came_adjoints[source]
        else:
            came = reply_adjoints[chip]
        cols = block_rows(source, lanes)
        _, log_second = order(total[:1, cols], near_total[:1, cols])
        _, second = order(adjoint[own, cols], near_adjoint[:, cols])
        moved = jnp.exp(log_second) * came + second
        leaving[own, cols] = jnp.where(is_first, moved, came)
        give_adjoint[:, cols] = jnp.where(is_first, came, moved)
        copy = remote(give_adjoint.at[:, cols], leaving.at[own, cols], la_send.at[source], la_recv.at[source], partner)
        copy.start()
        lasts.append(copy)
    for turn in range(1, chips):
        target = chip_of(turn)
        copy = remote(block, blocks.at[chip], spread_send.at[turn], spread_recv.at[chip], same_core(target))
        copy.start()
        sent.append(copy)
    blocks[chip] = block[...]
    for stream in range(4):
        gather(stream)
    for copy in lasts:
        copy.wait()

    def write_incoming(k, _):
        rows = block_rows(k, size)
        stack = jnp.concatenate(split2(behind[k, 0:1, :] * leaving[...]), axis=0)
        writes_part[rows, :] = writes_part[rows, :] + against(scaled_hi[k], scaled_lo[k], stack)
        return 0

    def out_copy(k):
        rows = block_rows(k, size)
        return pltpu.make_async_copy(x_all.at[rows, :], values_grad.at[rows, :], out_sem.at[k])

    def value_incoming(k, _):
        rows = block_rows(k, size)
        mine = stacks[k, 0:D_STATE, :].astype(F32) + stacks[k, D_STATE:, :].astype(F32)
        stack = jnp.concatenate(split2(mine + behind[k, 0:1, :] * leaving[...]), axis=0)
        b = writes[rows, :]
        outer = dot(jnp.concatenate([b, b], axis=1), stack)
        x_all[rows, :] = (inner[k] + outer * spread2(ends[k], spread)).astype(BF16)
        out_copy(k).start()
        return 0

    for stream in range(4):
        lax.fori_loop(2 * stream, 2 * stream + 2, write_incoming, 0, unroll=2)
        scatter(4 + stream)

    def value_steps(first, last):
        lax.fori_loop(first, last, value_incoming, 0)

    gather(4)
    value_steps(0, 1)
    gather(5)
    value_steps(1, 2)
    gather(6)
    value_steps(2, 3)
    gather(7)
    value_steps(3, 4)

    for turn in range(1, chips):
        source = chip_of(turn)
        remote(
            block, blocks.at[source], spread_send.at[turn], spread_recv.at[source], same_core(source)
        ).wait_recv()
    near_blocks = remote(blocks, whole.at[core], whole_send, whole_recv, partner)
    near_blocks.start()
    whole[core] = blocks[...]
    value_steps(4, count)

    near_blocks.wait()
    for k in range(chips):
        turned[k * lanes : (k + 1) * lanes, :] = jnp.concatenate([whole[0, k], whole[1, k]], axis=0).T
    for first in range(0, heads, 8):
        for p in range(HEAD_DIM):
            initial_out[first : first + 8, p * D_STATE : (p + 1) * D_STATE] = turned[
                pl.ds(first * HEAD_DIM + p, 8, stride=HEAD_DIM), :
            ]
    for copy in sent:
        copy.wait_send()
    for stream in range(8):
        for step in range(1, 4):
            direct(stream, step, 1).wait()
    for k in range(count):
        out_copy(k).wait()


def fused_part(values, writes, reads, grads, logs, start, chips):
    tokens, width = values.shape
    heads = logs.shape[0]
    count = tokens // CHUNK
    half = D_STATE // 2
    lanes = 2 * HEAD_DIM
    vmem = pl.BlockSpec(memory_space=pltpu.VMEM)
    hbm = pl.BlockSpec(memory_space=pl.ANY)
    dma = pltpu.SemaphoreType.DMA
    f32 = lambda *shape: pltpu.VMEM(shape, F32)
    bf16 = lambda *shape: pltpu.VMEM(shape, BF16)
    scratch = [
        bf16(tokens, width), bf16(tokens, width),
        f32(8, start.shape[1]), f32(D_STATE, lanes), f32(D_STATE, lanes),
        f32(count, CHUNK, heads), f32(count, CHUNK, heads), f32(count, CHUNK, heads),
        f32(count, heads, CHUNK), f32(count, 8, width), f32(count, 8, width),
        f32(D_STATE, width), f32(D_STATE, width), f32(8, width),
        f32(half, width), f32(half, width), f32(8, width),
        f32(chips, half + 8, lanes), f32(chips, half + 8, lanes),
        f32(chips, half, lanes), f32(chips, half, lanes),
        f32(chips, half, lanes), f32(chips, half, lanes),
        f32(chips, half, lanes), f32(chips, half, lanes),
        f32(half, width), f32(half, width),
        f32(D_STATE, width), f32(D_STATE, width),
        bf16(2 * D_STATE, width), bf16(count, 2 * D_STATE, width),
        bf16(count, CHUNK, width), bf16(count, CHUNK, width),
        f32(count, CHUNK, width),
        f32(tokens, D_STATE), f32(tokens, D_STATE),
        f32(8, 3, tokens // 16, D_STATE),
        f32(half, lanes), f32(chips, half, lanes), f32(2, chips, half, lanes),
        f32(heads * HEAD_DIM, D_STATE),
        dma((count,)), dma((count,)), dma, dma((3,)), dma((3,)),
        dma((chips,)), dma((chips,)), dma((chips,)), dma((chips,)),
        dma((chips,)), dma((chips,)), dma((chips,)), dma((chips,)),
        dma((chips,)), dma((chips,)), dma((chips,)), dma((chips,)),
        dma((48,)), dma((48,)), dma((chips,)), dma((chips,)), dma, dma, dma((count,)),
    ]
    return pl.pallas_call(
        fused_kernel,
        in_specs=[hbm, hbm, hbm, vmem, vmem, vmem],
        out_specs=[hbm, vmem, vmem, vmem],
        out_shape=[
            jax.ShapeDtypeStruct((tokens, width), BF16),
            jax.ShapeDtypeStruct((tokens, D_STATE), F32),
            jax.ShapeDtypeStruct((tokens, D_STATE), F32),
            jax.ShapeDtypeStruct((heads, HEAD_DIM * D_STATE), F32),
        ],
        scratch_shapes=scratch,
        compiler_params=pltpu.CompilerParams(collective_id=0, has_side_effects=True, vmem_limit_bytes=FUSED_LIMIT),
        cost_estimate=pl.CostEstimate(flops=2**34, bytes_accessed=20 * 2**20, transcendentals=0),
        name="fused_part",
    )(values, grads, start, writes, reads, logs)


PIECES = (8, 1, 1, 2)


def place_kernel(*refs):
    sources, targets, holds, in_sem, out_sem = refs[:4], refs[4:8], refs[8:12], refs[12], refs[13]
    ins, outs = [], []
    for source, target, hold, pieces in zip(sources, targets, holds, PIECES):
        rows = source.shape[0] // pieces
        for k in range(pieces):
            piece = pl.ds(k * rows, rows)
            ins.append(pltpu.make_async_copy(source.at[piece, :], hold.at[piece, :], in_sem.at[len(ins)]))
            outs.append(pltpu.make_async_copy(hold.at[piece, :], target.at[piece, :], out_sem.at[len(outs)]))
    for copy in ins:
        copy.start()
    for came, goes in zip(ins, outs):
        came.wait()
        goes.start()
    for copy in outs:
        copy.wait()


def place_part(*arrays):
    hbm = pl.BlockSpec(memory_space=pl.ANY)
    sems = pltpu.SemaphoreType.DMA((sum(PIECES),))
    return pl.pallas_call(
        place_kernel,
        in_specs=[hbm] * 4,
        out_specs=[hbm] * 4,
        out_shape=[jax.ShapeDtypeStruct(a.shape, a.dtype) for a in arrays],
        scratch_shapes=[pltpu.VMEM(a.shape, a.dtype) for a in arrays] + [sems, sems],
        compiler_params=pltpu.CompilerParams(vmem_limit_bytes=FUSED_LIMIT),
        cost_estimate=pl.CostEstimate(flops=0, bytes_accessed=12 * 2**20, transcendentals=0),
        name="place_part",
    )(*arrays)


def per_device(chips, values, writes, reads, out_grad, log_decay, starting_head_state):
    return place_part(*fused_part(values, writes, reads, out_grad, log_decay, starting_head_state, chips))


def solution(mesh):
    in_specs = (
        P("seq", "head"),
        P("seq", None),
        P("seq", None),
        P("seq", "head"),
        P("head", "seq"),
        P("head", None),
    )
    out_specs = (P("seq", "head"), P("seq", None), P("seq", None), P("head", None))
    chips = mesh.shape["seq"] // 2
    return jax.shard_map(
        functools.partial(per_device, chips), mesh=mesh, in_specs=in_specs, out_specs=out_specs, check_vma=False
    )
```
